512 devices in a mesh: tm: 16 (over y, core), space: 32 (over x, z).
Axes of the slice: x: 4, y: 8, z: 8, core: 2. Of those that a mesh axis runs over, the one named last changes fastest.
Arguments:
- video: bfloat16 [64, 32, 6, 20, 128], P('tm', 'space')
- conv_weight: bfloat16 [3, 3, 3, 3, 128, 128], replicated, may hold values from -0.109375 to 0.109375
- norm_gain: float32 [2, 128], replicated, may hold values from 0.1 to 1.9
- norm_bias: float32 [2, 128], replicated, may hold values from -3 to 3
Outputs:
- latent: bfloat16 [64, 32, 6, 20, 128], P('tm', 'space')
The draws below stay inside these ranges and needn't reach their ends.
All inputs are finite; a program needn't handle non-finite values.
Results may differ from the reference program's by a relative error of at most 0.006.
Values may be sent and summed in bfloat16 or wider, within the bound.
A program may use at most 64 MiB of HBM per device.

```python
import math
import jax
import jax.numpy as jnp
from jax import lax

C = 128
GROUPS = 32
TILE_COLS = 8
TW = 20
TH = 6
LAYERS = 3
FRAMES = 64
BANDS = 4
H = 24
W = 160


def draw_video(key, part):
    key = jax.random.fold_in(key, 11)
    key_base, key_cell, key_chan = jax.random.split(key, 3)
    rows = jnp.arange(H, dtype=jnp.float32)
    row_scale = jnp.exp(math.log(3.0) * rows / max(H - 1, 1))
    cell_scale = jnp.exp(jax.random.uniform(key_cell, (H, W), jnp.float32, 0.0, math.log(3.3)))
    chan_scale = jnp.exp(jax.random.uniform(key_chan, (C,), jnp.float32, 0.0, math.log(10.0))) / math.sqrt(10.0)
    scale = 0.4 * row_scale[:, None, None] * cell_scale[:, :, None] * chan_scale[None, None, :]
    base = jax.random.truncated_normal(key_base, -4.0, 4.0, (FRAMES, H, W, C), jnp.float32)
    whole = base * scale[None]
    split = whole.reshape(FRAMES, BANDS, TH, TILE_COLS, TW, C)
    tiled = split.transpose(0, 1, 3, 2, 4, 5).reshape(FRAMES, BANDS * TILE_COLS, TH, TW, C)
    return tiled.astype(jnp.bfloat16)


def normal_values(own_key, dims, scale, bound, held_as=jnp.bfloat16):
    return jnp.clip(scale * jax.random.normal(own_key, dims, jnp.float32), -bound, bound).astype(held_as)


def setup_inputs(seed: int = 0) -> dict:
    streams_of = jax.random.split(jax.random.key(seed), 5)
    return {
        "video": draw_video(jax.random.fold_in(streams_of[4], 71), 0),
        "conv_weight": normal_values(streams_of[1], (LAYERS, 3, 3, 3, C, C), (27 * C) ** -0.5, 0.109375),
        "norm_gain": jnp.clip(1.0 + 0.18 * jax.random.normal(streams_of[2], (LAYERS - 1, C), jnp.float32), 0.1, 1.9),
        "norm_bias": normal_values(streams_of[3], (LAYERS - 1, C), 0.5, 3.0, jnp.float32),
    }


EPS = 1e-05

def taps(block, weight):
    frames = block.shape[0] - 2
    rows = block.shape[1] - 2
    width = block.shape[2] - 2
    chans = block.shape[3]
    kernel = weight.reshape(3, 3, 3 * chans, chans)
    total = jnp.zeros((frames * rows * width, chans), jnp.float32)
    for step_t in range(3):
        for step_r in range(3):
            columns = jnp.concatenate([block[step_t:step_t + frames, step_r:step_r + rows, step_c:step_c + width] for step_c in range(3)], axis=-1)
            total = total + jnp.dot(columns.reshape(-1, 3 * chans), kernel[step_t, step_r], preferred_element_type=jnp.float32)
    return total.reshape(frames, rows, width, chans)

def group_norm(frame_out, gain, bias):
    chans = frame_out.shape[-1]
    per = chans // GROUPS
    count = frame_out.shape[0] * frame_out.shape[1] * per
    first = lax.optimization_barrier(jnp.sum(frame_out, axis=(0, 1))).reshape(GROUPS, per).sum(-1)
    second = lax.optimization_barrier(jnp.sum(frame_out * frame_out, axis=(0, 1))).reshape(GROUPS, per).sum(-1)
    mean = first / count
    var = second / count - mean * mean
    mean_c = jnp.repeat(mean, per)
    scale_c = jnp.repeat(lax.rsqrt(var + EPS), per)
    return jax.nn.silu((frame_out - mean_c) * scale_c * gain + bias).astype(jnp.bfloat16)

def to_frames(tiled):
    frames = tiled.shape[0]
    split = tiled.reshape(frames, BANDS, TILE_COLS, TH, TW, C)
    return split.transpose(0, 1, 3, 2, 4, 5).reshape(frames, BANDS * TH, TILE_COLS * TW, C)

def to_tiles(whole):
    frames = whole.shape[0]
    split = whole.reshape(frames, BANDS, TH, TILE_COLS, TW, C)
    return split.transpose(0, 1, 3, 2, 4, 5).reshape(frames, BANDS * TILE_COLS, TH, TW, C)

def reference(video, conv_weight, norm_gain, norm_bias):
    current = to_frames(video)
    frames_all = current.shape[0]
    for layer in range(LAYERS):
        padded = jnp.pad(current, ((2, 0), (1, 1), (1, 1), (0, 0)))
        weight = conv_weight[layer]
        last = layer == LAYERS - 1

        def one_frame(index):
            slab = lax.dynamic_slice_in_dim(padded, index, 3, 0)
            result = taps(slab, weight)[0]
            if last:
                return result.astype(jnp.bfloat16)
            return group_norm(result, norm_gain[layer], norm_bias[layer])
        current = lax.map(one_frame, jnp.arange(frames_all, dtype=jnp.int32))
    return to_tiles(current)
```

```python
import jax
import jax.numpy as jnp
from jax import lax
from jax.experimental import pallas as pl
from jax.experimental.pallas import tpu as pltpu
from jax.sharding import PartitionSpec as P

GROUPS = 32
TILE_COLS = 8
BANDS = 4
LAYERS = 3
EPS = 1e-05
F32 = jnp.float32
BF16 = jnp.bfloat16
MESH = pl.DeviceIdType.MESH

FR = 4
TH = 6
TW = 20
C = 128
CELLS = TH * TW
ROWS = 128
PAD = 8
XROWS = PAD + (TH + 2) * TW + 8
K = 9 * C
COUNT = BANDS * TH * TILE_COLS * TW * (C // GROUPS)


def dot(left, right):
    return jnp.dot(left, right, preferred_element_type=F32)


def pack_sums(total):
    lane = lax.broadcasted_iota(jnp.int32, (1, C), 1) % 4
    pair = total + pltpu.roll(total, 1, 1)
    quad = pair + pltpu.roll(pair, 2, 1)
    first = jnp.zeros((1, C), F32)
    second = jnp.zeros((1, C), F32)
    for f in range(FR):
        moved = quad if f == 3 else pltpu.roll(quad, C - (3 - f), 1)
        first = jnp.where(lane == f, moved[f : f + 1], first)
        second = jnp.where(lane == f, moved[4 + f : 5 + f], second)
    return jnp.concatenate([first, second], axis=0)


def unpack_sums(packed):
    lane = lax.broadcasted_iota(jnp.int32, (8, C), 1) % 4
    row = lax.broadcasted_iota(jnp.int32, (8, C), 0)
    spread = jnp.where(row < 4, packed[0:1], packed[1:2])
    only = jnp.where(lane == row % 4, spread, 0.0)
    lead = jnp.where(row % 4 == 0, only, 0.0)
    for f in range(1, FR):
        lead = jnp.where(row % 4 == f, pltpu.roll(only, C - f, 1), lead)
    pair = lead + pltpu.roll(lead, 1, 1)
    return pair + pltpu.roll(pair, 2, 1)


def moments(packed, gain):
    sums = unpack_sums(packed) * (1.0 / COUNT)
    mean = sums[0:4]
    var = sums[4:8] - mean * mean
    return mean, lax.rsqrt(var + EPS) * gain


def kernel(
    video,
    weights,
    gain_in,
    bias_in,
    out,
    w,
    vid,
    gains,
    biases,
    y,
    acc,
    xc,
    im,
    cols,
    corners,
    rim,
    rim_corner,
    halo,
    halo_rim,
    halo_corner,
    packed,
    slots,
    prev_slots,
    load_sem,
    send_sem,
    recv_sem,
    stat_send,
    stat_recv,
):
    tm = lax.axis_index("tm")
    space = lax.axis_index("space")
    n_tm = lax.axis_size("tm")
    n_space = lax.axis_size("space")
    band = space // TILE_COLS
    column = space % TILE_COLS
    up = lax.rem(band + BANDS - 1, BANDS)
    down = lax.rem(band + 1, BANDS)
    left = lax.rem(column + TILE_COLS - 1, TILE_COLS)
    right = lax.rem(column + 1, TILE_COLS)
    after = lax.rem(tm + 1, n_tm)
    before = lax.rem(tm + n_tm - 1, n_tm)

    loads = [pltpu.make_async_copy(video, vid, load_sem.at[0])]
    for layer in range(LAYERS):
        loads.append(pltpu.make_async_copy(weights.at[layer], w.at[layer], load_sem.at[1 + layer]))
    loads.append(pltpu.make_async_copy(gain_in, gains, load_sem.at[4]))
    loads.append(pltpu.make_async_copy(bias_in, biases, load_sem.at[5]))
    for copy in loads:
        copy.start()

    barrier = pltpu.get_barrier_semaphore()

    def greet(d, carry):
        pl.semaphore_signal(barrier, inc=1, device_id=(before, lax.rem(space + d, n_space)), device_id_type=MESH)

        @pl.when(d > 0)
        def _():
            pl.semaphore_signal(barrier, inc=1, device_id=(tm, lax.rem(space + d, n_space)), device_id_type=MESH)

        return carry

    lax.fori_loop(0, n_space, greet, 0)

    loads[0].wait()
    for f in range(FR):
        for h in range(TH):
            y[0, f, h * TW : (h + 1) * TW, :] = vid[f, h].astype(F32)
    pl.semaphore_wait(barrier, 2 * n_space - 1)

    row8 = lax.broadcasted_iota(jnp.int32, (8, C), 0)
    pending = []

    def send(t, k, source, target, device):
        copy = pltpu.make_async_remote_copy(
            src_ref=source,
            dst_ref=target,
            send_sem=send_sem.at[t, k],
            recv_sem=recv_sem.at[t, 0 if k < 4 else (1 if k < 8 else k - 6)],
            device_id=device,
            device_id_type=MESH,
        )
        copy.start()
        pending.append(copy)

    def arrived(t, k, buffer):
        pltpu.make_async_copy(buffer, buffer, recv_sem.at[t, k]).wait()

    def fill(slot, own, top, bottom, left_side, right_side):
        for c in range(3):
            off = PAD + 1 - c
            xc[slot, c, off : off + TW, :] = top
            xc[slot, c, off + TW : off + TW + CELLS, :] = own
            xc[slot, c, off + TW + CELLS : off + 2 * TW + CELLS, :] = bottom
        xc[slot, 0, pl.ds(PAD, TH + 2, stride=TW), :] = left_side
        xc[slot, 2, pl.ds(PAD + TW - 1, TH + 2, stride=TW), :] = right_side
        zeros = jnp.zeros((ROWS - CELLS, C), F32)
        for b in range(3):
            for c in range(3):
                start = PAD + b * TW
                part = jnp.concatenate([xc[slot, c, start : start + CELLS, :], zeros], axis=0)
                tap = b * 3 + c
                im[slot, :, tap * C : (tap + 1) * C] = part.astype(BF16)

    def side(column_part, top_corner, bottom_corner, keep):
        value = jnp.where(row8 == 0, top_corner, jnp.where(row8 == TH + 1, bottom_corner, column_part))
        return value, keep & ((row8 > 0) | (band > 0)) & ((row8 < TH + 1) | (band < BANDS - 1))

    def frame(slot, own, rims, corner_rows, act, keep):
        left_side, keep_left = side(rims[48:56], corner_rows[0], corner_rows[2], column > 0)
        right_side, keep_right = side(rims[56:64], corner_rows[1], corner_rows[3], column < TILE_COLS - 1)
        fill(
            slot,
            keep(act(own)),
            keep(jnp.where(band > 0, act(rims[4:24]), 0.0)),
            keep(jnp.where(band < BANDS - 1, act(rims[24:44]), 0.0)),
            keep(jnp.where(keep_left, act(left_side), 0.0)),
            keep(jnp.where(keep_right, act(right_side), 0.0)),
        )

    for t in range(LAYERS):
        s = t - 1
        if t > 0:
            value = y[t]
            sums = [jnp.sum(value[f], axis=0, keepdims=True) for f in range(FR)]
            squares = [jnp.sum(value[f] * value[f], axis=0, keepdims=True) for f in range(FR)]
            packed[s] = pack_sums(jnp.concatenate(sums + squares, axis=0))

            def tell(d, carry, s=s):
                pltpu.make_async_remote_copy(
                    src_ref=packed.at[s],
                    dst_ref=slots.at[s, d - 1],
                    send_sem=stat_send.at[s, 0],
                    recv_sem=stat_recv.at[s, 0],
                    device_id=(tm, lax.rem(space + d, n_space)),
                    device_id_type=MESH,
                ).start()
                return carry

            lax.fori_loop(1, n_space, tell, 0)

        for f in range(FR):
            cols[t, 0, f, 1 : TH + 1, :] = y[t, f, pl.ds(0, TH, stride=TW), :]
            cols[t, 1, f, 1 : TH + 1, :] = y[t, f, pl.ds(TW - 1, TH, stride=TW), :]
            for k, cell in enumerate((0, TW - 1, (TH - 1) * TW, CELLS - 1)):
                corners[t, k, f : f + 1, :] = y[t, f, cell : cell + 1, :]
        send(t, 0, y.at[t, :, 96:120], rim.at[t, :, 0:24], (tm, down * TILE_COLS + column))
        send(t, 1, y.at[t, :, 0:24], rim.at[t, :, 24:48], (tm, up * TILE_COLS + column))
        send(t, 2, cols.at[t, 1], rim.at[t, :, 48:56], (tm, band * TILE_COLS + right))
        send(t, 3, cols.at[t, 0], rim.at[t, :, 56:64], (tm, band * TILE_COLS + left))
        send(t, 4, corners.at[t, 0], rim_corner.at[t, 3], (tm, up * TILE_COLS + left))
        send(t, 5, corners.at[t, 1], rim_corner.at[t, 2], (tm, up * TILE_COLS + right))
        send(t, 6, corners.at[t, 2], rim_corner.at[t, 1], (tm, down * TILE_COLS + left))
        send(t, 7, corners.at[t, 3], rim_corner.at[t, 0], (tm, down * TILE_COLS + right))
        send(t, 8, y.at[t, 2:4], halo.at[t], (after, space))

        if t > 0:

            def tell_next(d, carry, s=s):
                pltpu.make_async_remote_copy(
                    src_ref=packed.at[s],
                    dst_ref=prev_slots.at[s, d],
                    send_sem=stat_send.at[s, 1],
                    recv_sem=stat_recv.at[s, 1],
                    device_id=(after, lax.rem(space + d, n_space)),
                    device_id_type=MESH,
                ).start()
                return carry

            lax.fori_loop(0, n_space, tell_next, 0)

        arrived(t, 0, rim.at[t])
        arrived(t, 1, rim_corner.at[t])
        send(t, 9, rim.at[t, 2:4], halo_rim.at[t], (after, space))
        send(t, 10, rim_corner.at[t], halo_corner.at[t], (after, space))

        if t == 0:
            loads[1].wait()

            def act_of(f, stats):
                return lambda value: value

            stats = None
        else:
            if t == 1:
                loads[4].wait()
                loads[5].wait()
            loads[1 + t].wait()
            gain = gains[s : s + 1, :]
            bias = biases[s : s + 1, :]

            def act_of(f, stats, bias=bias):
                mean, scale = stats

                def act(value):
                    v = (value - mean[f : f + 1]) * scale[f : f + 1] + bias
                    return v / (1.0 + jnp.exp(-v))

                return act

            pltpu.make_async_copy(slots.at[s], slots.at[s], stat_recv.at[s, 0]).wait()
            stats = moments(packed[s] + jnp.sum(slots[s], axis=0), gain)

        for f in range(FR):
            frame(
                2 + f,
                y[t, f, 0:CELLS, :],
                rim[t, f],
                [rim_corner[t, k, f : f + 1, :] for k in range(4)],
                act_of(f, stats),
                lambda value: value,
            )
        w21 = jnp.concatenate([w[t, 2], w[t, 1]], axis=1)
        two = dot(im[2:5].reshape(3 * ROWS, K), w21).reshape(3, ROWS, 2 * C)
        one = dot(im[5], w[t, 2])
        old = dot(im[2:4].reshape(2 * ROWS, K), w[t, 0]).reshape(2, ROWS, C)
        acc[0] = two[0, :, :C]
        acc[1] = two[0, :, C:] + two[1, :, :C]
        acc[2] = two[1, :, C:] + two[2, :, :C] + old[0]
        acc[3] = two[2, :, C:] + one + old[1]

        if t > 0:
            pltpu.make_async_copy(prev_slots.at[s], prev_slots.at[s], stat_recv.at[s, 1]).wait()
            stats = moments(jnp.sum(prev_slots[s], axis=0), gain)
        arrived(t, 2, halo.at[t])
        arrived(t, 3, halo_rim.at[t])
        arrived(t, 4, halo_corner.at[t])
        for f in range(2):
            frame(
                f,
                halo[t, f, 0:CELLS, :],
                halo_rim[t, f],
                [halo_corner[t, k, 2 + f : 3 + f, :] for k in range(4)],
                act_of(2 + f, stats),
                lambda value: jnp.where(tm > 0, value, 0.0),
            )
        w10 = jnp.concatenate([w[t, 1], w[t, 0]], axis=1)
        near = dot(im[1], w10)
        far = dot(im[0], w[t, 0])
        result = [acc[0] + near[:, :C] + far, acc[1] + near[:, C:], acc[2], acc[3]]
        for f in range(FR):
            if t < LAYERS - 1:
                y[t + 1, f] = result[f]
            else:
                for h in range(TH):
                    out[f, h] = result[f][h * TW : (h + 1) * TW].astype(BF16)

    for copy in pending:
        copy.wait_send()
    for s in range(LAYERS - 1):
        pltpu.make_async_copy(slots.at[s], slots.at[s], stat_send.at[s, 0]).wait()
        pltpu.make_async_copy(prev_slots.at[s], prev_slots.at[s], stat_send.at[s, 1]).wait()


def on_device(video, conv_weight, norm_gain, norm_bias):
    n_space = lax.axis_size("space")
    any_spec = pl.BlockSpec(memory_space=pl.ANY)
    result = pl.pallas_call(
        kernel,
        out_shape=jax.ShapeDtypeStruct((FR, TH, TW, C), BF16),
        in_specs=[any_spec] * 4,
        out_specs=pl.BlockSpec(memory_space=pltpu.VMEM),
        scratch_shapes=[
            pltpu.VMEM((LAYERS, 3, K, C), BF16),
            pltpu.VMEM((FR, TH, TW, C), BF16),
            pltpu.VMEM((LAYERS - 1, C), F32),
            pltpu.VMEM((LAYERS - 1, C), F32),
            pltpu.VMEM((LAYERS, FR, ROWS, C), F32),
            pltpu.VMEM((FR, ROWS, C), F32),
            pltpu.VMEM((FR + 2, 3, XROWS, C), F32),
            pltpu.VMEM((FR + 2, ROWS, K), BF16),
            pltpu.VMEM((LAYERS, 2, FR, 8, C), F32),
            pltpu.VMEM((LAYERS, 4, 8, C), F32),
            pltpu.VMEM((LAYERS, FR, 64, C), F32),
            pltpu.VMEM((LAYERS, 4, 8, C), F32),
            pltpu.VMEM((LAYERS, 2, ROWS, C), F32),
            pltpu.VMEM((LAYERS, 2, 64, C), F32),
            pltpu.VMEM((LAYERS, 4, 8, C), F32),
            pltpu.VMEM((LAYERS - 1, 2, C), F32),
            pltpu.VMEM((LAYERS - 1, n_space - 1, 2, C), F32),
            pltpu.VMEM((LAYERS - 1, n_space, 2, C), F32),
            pltpu.SemaphoreType.DMA((6,)),
            pltpu.SemaphoreType.DMA((LAYERS, 11)),
            pltpu.SemaphoreType.DMA((LAYERS, 5)),
            pltpu.SemaphoreType.DMA((LAYERS - 1, 2)),
            pltpu.SemaphoreType.DMA((LAYERS - 1, 2)),
        ],
        compiler_params=pltpu.CompilerParams(
            collective_id=0, has_side_effects=True, vmem_limit_bytes=48 << 20
        ),
        cost_estimate=pl.CostEstimate(flops=1274019840, bytes_accessed=2900000, transcendentals=300000),
        name="conv_stack",
    )(
        video.reshape(FR, TH, TW, C),
        conv_weight.reshape(LAYERS, 3, K, C),
        norm_gain,
        norm_bias,
    )
    return result[:, None]


def solution(mesh):
    placed = (P("tm", "space", None, None, None), P(), P(), P())
    return jax.shard_map(
        on_device,
        mesh=mesh,
        in_specs=placed,
        out_specs=P("tm", "space", None, None, None),
        check_vma=False,
    )
```

```python
import jax
import jax.numpy as jnp
from jax import lax
from jax.experimental import pallas as pl
from jax.experimental.pallas import tpu as pltpu
from jax.sharding import PartitionSpec as P

GROUPS = 32
TILE_COLS = 8
BANDS = 4
LAYERS = 3
EPS = 1e-05
F32 = jnp.float32
BF16 = jnp.bfloat16
MESH = pl.DeviceIdType.MESH

FR = 4
TH = 6
TW = 20
C = 128
CELLS = TH * TW
ROWS = 128
PAD = 8
XROWS = PAD + (TH + 2) * TW + 8
K = 9 * C
COUNT = BANDS * TH * TILE_COLS * TW * (C // GROUPS)


def dot(left, right):
    return jnp.dot(left, right, preferred_element_type=F32)


def pack_sums(total):
    lane = lax.broadcasted_iota(jnp.int32, (1, C), 1) % 4
    pair = total + pltpu.roll(total, 1, 1)
    quad = pair + pltpu.roll(pair, 2, 1)
    first = jnp.zeros((1, C), F32)
    second = jnp.zeros((1, C), F32)
    for f in range(FR):
        moved = quad if f == 3 else pltpu.roll(quad, C - (3 - f), 1)
        first = jnp.where(lane == f, moved[f : f + 1], first)
        second = jnp.where(lane == f, moved[4 + f : 5 + f], second)
    return jnp.concatenate([first, second], axis=0)


def unpack_sums(packed):
    lane = lax.broadcasted_iota(jnp.int32, (8, C), 1) % 4
    row = lax.broadcasted_iota(jnp.int32, (8, C), 0)
    spread = jnp.where(row < 4, packed[0:1], packed[1:2])
    only = jnp.where(lane == row % 4, spread, 0.0)
    lead = jnp.where(row % 4 == 0, only, 0.0)
    for f in range(1, FR):
        lead = jnp.where(row % 4 == f, pltpu.roll(only, C - f, 1), lead)
    pair = lead + pltpu.roll(lead, 1, 1)
    return pair + pltpu.roll(pair, 2, 1)


def moments(packed, gain):
    sums = unpack_sums(packed) * (1.0 / COUNT)
    mean = sums[0:4]
    var = sums[4:8] - mean * mean
    return mean, lax.rsqrt(var + EPS) * gain


def side(column_part, top_corner, bottom_corner):
    row = lax.broadcasted_iota(jnp.int32, (8, C), 0)
    return jnp.where(row == 0, top_corner, jnp.where(row == TH + 1, bottom_corner, column_part))


def far_first(i):
    k = i // 4
    return lax.rem(2 + 3 * lax.rem(i, 4), BANDS), lax.rem(4 + (k + 1) // 2 * (2 * lax.rem(k, 2) - 1), TILE_COLS)


SELF = 30

STEPS = ((1, 0), (-1, 0), (0, 1), (0, -1), (-1, -1), (-1, 1), (1, -1), (1, 1))
CORNERS = ((0, 0), (0, TW - 1), (TH - 1, 0), (TH - 1, TW - 1))


def kernel(
    video,
    weights,
    gain_in,
    bias_in,
    out,
    w,
    vid,
    inter,
    first_row,
    first_col,
    first_corner,
    row_cells,
    col_cells,
    gains,
    biases,
    y,
    acc,
    xc,
    im,
    stage_row,
    stage_col,
    stage_corner,
    out_row,
    out_col,
    out_corner,
    out_halo,
    in_row,
    in_col,
    in_corner,
    next_row,
    next_col,
    next_corner,
    halo,
    rim_row,
    rim_col,
    rim_corner,
    packed,
    slots,
    prev_slots,
    load_sem,
    send_sem,
    recv_sem,
    stat_send,
    stat_recv,
    near_sem,
    ready_sem,
):
    tm = lax.axis_index("tm")
    space = lax.axis_index("space")
    n_tm = lax.axis_size("tm")
    n_space = lax.axis_size("space")
    band = space // TILE_COLS
    column = lax.rem(space, TILE_COLS)
    after = lax.rem(tm + 1, n_tm)
    before = lax.rem(tm + n_tm - 1, n_tm)

    def tile(bands, columns):
        return lax.rem(band + bands + BANDS, BANDS) * TILE_COLS + lax.rem(column + columns + TILE_COLS, TILE_COLS)

    barrier = pltpu.get_barrier_semaphore()
    for step in STEPS:
        pl.semaphore_signal(barrier, inc=1, device_id=(tm, tile(*step)), device_id_type=MESH)
    for step in ((0, 0),) + STEPS:
        pl.semaphore_signal(barrier, inc=1, device_id=(before, tile(*step)), device_id_type=MESH)

    loads = [pltpu.make_async_copy(video, vid, load_sem.at[0])]
    for layer in range(LAYERS):
        loads.append(pltpu.make_async_copy(weights.at[layer], w.at[layer], load_sem.at[1 + layer]))
    loads.append(pltpu.make_async_copy(gain_in, gains, load_sem.at[4]))
    loads.append(pltpu.make_async_copy(bias_in, biases, load_sem.at[5]))
    for copy in loads:
        copy.start()
    loads[0].wait()
    inter[...] = vid[...].astype(F32).reshape(FR * CELLS, C)
    for f in range(2):
        whole = jnp.concatenate([inter[pl.ds(2 + f, CELLS, stride=FR), :], jnp.zeros((ROWS - CELLS, C), F32)], axis=0)
        out_halo[0, f] = whole.astype(BF16)
    pl.semaphore_wait(barrier, 2 * len(STEPS) + 1)

    sent = {}

    def send(t, k, source, target, device):
        copy = pltpu.make_async_remote_copy(
            src_ref=source,
            dst_ref=target,
            send_sem=send_sem.at[t, k],
            recv_sem=recv_sem.at[t, k],
            device_id=device,
            device_id_type=MESH,
        )
        copy.start()
        sent[t, k] = copy

    def fill(slot, own, top, bottom, left_side, right_side):
        for c in range(3):
            off = PAD + 1 - c
            xc[slot, c, off : off + TW, :] = top
            xc[slot, c, off + TW : off + TW + CELLS, :] = own
            xc[slot, c, off + TW + CELLS : off + 2 * TW + CELLS, :] = bottom
        xc[slot, 0, pl.ds(PAD, TH + 2, stride=TW), :] = left_side
        xc[slot, 2, pl.ds(PAD + TW - 1, TH + 2, stride=TW), :] = right_side
        zeros = jnp.zeros((ROWS - CELLS, C), F32)
        for b in range(3):
            for c in range(3):
                start = PAD + b * TW
                part = jnp.concatenate([xc[slot, c, start : start + CELLS, :], zeros], axis=0)
                tap = b * 3 + c
                im[slot, :, tap * C : (tap + 1) * C] = part.astype(BF16)

    row8 = lax.broadcasted_iota(jnp.int32, (8, C), 0)
    keep_rows = ((row8 > 0) | (band > 0)) & ((row8 < TH + 1) | (band < BANDS - 1))
    keep_left = keep_rows & (column > 0)
    keep_right = keep_rows & (column < TILE_COLS - 1)

    def frame(slot, parts, act, keep):
        own, top, bottom, left_side, right_side = (act(*part) for part in parts)
        fill(
            slot,
            keep(own),
            keep(jnp.where(band > 0, top, 0.0)),
            keep(jnp.where(band < BANDS - 1, bottom, 0.0)),
            keep(jnp.where(keep_left, left_side, 0.0)),
            keep(jnp.where(keep_right, right_side, 0.0)),
        )

    def same(value, shift=None):
        return value

    def later(value):
        return jnp.where(tm > 0, value, 0.0)

    def split(g, f):
        return (
            (row_cells[g, 0, pl.ds(f, TW, stride=FR), :], None),
            (row_cells[g, 1, pl.ds(f, TW, stride=FR), :], None),
            (col_cells[g, 0, pl.ds(f, TH + 2, stride=FR), :], None),
            (col_cells[g, 1, pl.ds(f, TH + 2, stride=FR), :], None),
        )

    def unpack_rims(g):
        for i in range(2):
            row_cells[g, i] = first_row[g, i].astype(F32).reshape(FR * TW, C)
            col_cells[g, i, FR : FR * (TH + 1), :] = first_col[g, i].astype(F32).reshape(FR * TH, C)
            col_cells[g, i, 0:FR, :] = first_corner[g, i].astype(F32).reshape(FR, C)
            col_cells[g, i, FR * (TH + 1) :, :] = first_corner[g, 2 + i].astype(F32).reshape(FR, C)

    def rims_of(p, f):
        lo = f * TW
        own = 2 * p + f
        rims = [(rim_row[i, p, lo : lo + TW, :], rim_row[i, p, 2 * TW + f : 2 * TW + f + 1, :]) for i in range(2)]
        for i in range(2):
            part = rim_col[i, p, 8 * f : 8 * f + 8, :]
            upper, lower = ((rim_corner[k, 0, own : own + 1, :], rim_corner[k, 1, own : own + 1, :]) for k in (i, 2 + i))
            rims.append((side(part, upper[0], lower[0]), side(part[0:1], upper[1], lower[1])))
        return rims

    for t in range(LAYERS):
        s = t - 1
        if t == 0:
            rims = [vid.at[TH - 1], vid.at[0], vid.at[:, TW - 1], vid.at[:, 0]] + [vid.at[h, pl.ds(c, 1)] for h, c in CORNERS]
            for g, where_to in ((0, tm), (1, after)):
                lands = [first_row.at[g, 0], first_row.at[g, 1], first_col.at[g, 0], first_col.at[g, 1]] + [
                    first_corner.at[g, 3 - k] for k in range(4)
                ]
                for k, step in enumerate(STEPS):
                    send(0, 9 * g + k, rims[k], lands[k], (where_to, tile(*step)))
                if g == 0:
                    send(0, 8, out_halo.at[0], halo.at[0], (after, space))
        else:
            value = y[s]
            sums = [jnp.sum(value[f], axis=0, keepdims=True) for f in range(FR)]
            squares = [jnp.sum(value[f] * value[f], axis=0, keepdims=True) for f in range(FR)]
            packed[s] = pack_sums(jnp.concatenate(sums + squares, axis=0))

            def tell(i, slot, s=s):
                pltpu.make_async_remote_copy(
                    src_ref=packed.at[s],
                    dst_ref=slots.at[s, slot],
                    send_sem=stat_send.at[s, 0],
                    recv_sem=stat_recv.at[s, 0],
                    device_id=(tm, tile(*far_first(i))),
                    device_id_type=MESH,
                ).start()

            def tell_next(i, carry, s=s):
                pltpu.make_async_remote_copy(
                    src_ref=packed.at[s],
                    dst_ref=prev_slots.at[s, i],
                    send_sem=stat_send.at[s, 1],
                    recv_sem=stat_recv.at[s, 1],
                    device_id=(after, tile(*far_first(i))),
                    device_id_type=MESH,
                ).start()
                return carry

            def tell_one(i, carry, tell=tell):
                tell(i, i)
                return carry

            lax.fori_loop(0, SELF, tell_one, 0)
            tell(SELF + 1, SELF)
            if t == 1:
                pl.semaphore_wait(ready_sem, 1)
            lax.fori_loop(0, n_space, tell_next, 0)

            for f in range(FR):
                off = (sums[f] * (1.0 / CELLS)).astype(BF16).astype(F32)
                p, lo = f // 2, f % 2
                for i, first in enumerate((CELLS - TW, 0)):
                    stage_row[i, p, lo * TW : (lo + 1) * TW, :] = y[s, f, first : first + TW, :] - off
                    stage_row[i, p, 2 * TW + lo : 2 * TW + lo + 1, :] = off
                for i, first in enumerate((TW - 1, 0)):
                    stage_col[i, p, 8 * lo : 8 * lo + 8, :] = jnp.broadcast_to(off, (8, C))
                    stage_col[i, p, 8 * lo + 1 : 8 * lo + 1 + TH, :] = y[s, f, pl.ds(first, TH, stride=TW), :] - off
                for k, (h, c) in enumerate(CORNERS):
                    cell = h * TW + c
                    stage_corner[k, 0, f : f + 1, :] = y[s, f, cell : cell + 1, :] - off
                    stage_corner[k, 1, f : f + 1, :] = off
                if p == 1:
                    whole = jnp.concatenate([y[s, f, 0:CELLS, :] - off, jnp.broadcast_to(off, (ROWS - CELLS, C))], axis=0)
                    out_halo[t, lo] = whole.astype(BF16)
            out_row[s] = stage_row[...].astype(BF16)
            out_col[s] = stage_col[...].astype(BF16)
            out_corner[s] = stage_corner[...].astype(BF16)
            for k, step in enumerate(STEPS):
                if k < 2:
                    source, land = out_row.at[s, k], in_row.at[s, k]
                elif k < 4:
                    source, land = out_col.at[s, k - 2], in_col.at[s, k - 2]
                else:
                    source, land = out_corner.at[s, k - 4], in_corner.at[s, 7 - k]
                send(t, k, source, land, (tm, tile(*step)))
            send(t, 8, out_halo.at[t], halo.at[t], (after, space))
            for k, step in enumerate(STEPS):
                if k < 2:
                    source, land = out_row.at[s, k, 1], next_row.at[s, k]
                elif k < 4:
                    source, land = out_col.at[s, k - 2, 1], next_col.at[s, k - 2]
                else:
                    source, land = out_corner.at[s, k - 4], next_corner.at[s, 7 - k]
                send(t, 9 + k, source, land, (after, tile(*step)))

        for k in range(8):
            sent[t, k].wait_recv()
        loads[1 + t].wait()

        if t == 0:
            for columns in (2, -2):
                pl.semaphore_signal(near_sem, inc=1, device_id=(tm, tile(0, columns)), device_id_type=MESH)
            unpack_rims(0)
            for f in range(FR):
                frame(2 + f, [(inter[pl.ds(f, CELLS, stride=FR), :], None), *split(0, f)], same, same)
        else:
            if t == 1:
                loads[4].wait()
                loads[5].wait()
            gain = gains[s : s + 1, :]
            bias = biases[s : s + 1, :]

            def act_of(f, stats, bias=bias):
                mean, scale = stats

                def act(value, off=0.0):
                    v = (value + (off - mean[f : f + 1])) * scale[f : f + 1] + bias
                    return v / (1.0 + jnp.exp(-v))

                return act

            rim_row[...] = in_row[s].astype(F32)
            rim_col[...] = in_col[s].astype(F32)
            rim_corner[...] = in_corner[s].astype(F32)
            pltpu.make_async_copy(slots.at[s], slots.at[s], stat_recv.at[s, 0]).wait()
            stats = moments(packed[s] + jnp.sum(slots[s], axis=0), gain)
            for f in range(FR):
                frame(2 + f, [(y[s, f, 0:CELLS, :],), *rims_of(f // 2, f % 2)], act_of(f, stats), same)

        w21 = jnp.concatenate([w[t, 2], w[t, 1]], axis=1)
        two = dot(im[2:5].reshape(3 * ROWS, K), w21).reshape(3, ROWS, 2 * C)
        one = dot(im[5], w[t, 2])
        old = dot(im[2:4].reshape(2 * ROWS, K), w[t, 0]).reshape(2, ROWS, C)
        acc[0] = two[0, :, :C]
        acc[1] = two[0, :, C:] + two[1, :, :C]
        acc[2] = two[1, :, C:] + two[2, :, :C] + old[0]
        acc[3] = two[2, :, C:] + one + old[1]

        for k in range(8, 17):
            sent[t, k].wait_recv()
        if t == 0:
            pl.semaphore_wait(near_sem, 2)
            pl.semaphore_signal(ready_sem, inc=1, device_id=(before, space), device_id_type=MESH)
            unpack_rims(1)
            for f in range(2):
                frame(f, [(halo[0, f].astype(F32)[0:CELLS],), *split(1, 2 + f)], same, later)
        else:
            for i in range(2):
                rim_row[i, 1] = next_row[s, i].astype(F32)
                rim_col[i, 1] = next_col[s, i].astype(F32)
            rim_corner[...] = next_corner[s].astype(F32)
            pltpu.make_async_copy(prev_slots.at[s], prev_slots.at[s], stat_recv.at[s, 1]).wait()
            stats = moments(jnp.sum(prev_slots[s], axis=0), gain)
            for f in range(2):
                whole = halo[t, f].astype(F32)
                frame(f, [(whole[0:CELLS], whole[CELLS : CELLS + 1]), *rims_of(1, f)], act_of(2 + f, stats), later)
        w10 = jnp.concatenate([w[t, 1], w[t, 0]], axis=1)
        near = dot(im[1], w10)
        far = dot(im[0], w[t, 0])
        result = [acc[0] + near[:, :C] + far, acc[1] + near[:, C:], acc[2], acc[3]]
        for f in range(FR):
            if t < LAYERS - 1:
                y[t, f] = result[f]
            else:
                for h in range(TH):
                    out[f, h] = result[f][h * TW : (h + 1) * TW].astype(BF16)

    for copy in sent.values():
        copy.wait_send()
    for s in range(LAYERS - 1):
        pltpu.make_async_copy(slots.at[s], slots.at[s], stat_send.at[s, 0]).wait()
        pltpu.make_async_copy(prev_slots.at[s], prev_slots.at[s], stat_send.at[s, 1]).wait()


def on_device(video, conv_weight, norm_gain, norm_bias):
    n_space = lax.axis_size("space")
    inner = LAYERS - 1
    arguments = (
        video.reshape(FR, TH, TW, C).transpose(1, 2, 0, 3),
        conv_weight.reshape(LAYERS, 3, K, C),
        norm_gain,
        norm_bias,
    )
    result = pl.pallas_call(
        kernel,
        out_shape=jax.ShapeDtypeStruct((FR, TH, TW, C), BF16),
        in_specs=[pl.BlockSpec(memory_space=pltpu.HBM)] * 4,
        out_specs=pl.BlockSpec(memory_space=pltpu.VMEM),
        scratch_shapes=[
            pltpu.VMEM((LAYERS, 3, K, C), BF16),
            pltpu.VMEM((TH, TW, FR, C), BF16),
            pltpu.VMEM((FR * CELLS, C), F32),
            pltpu.VMEM((2, 2, TW, FR, C), BF16),
            pltpu.VMEM((2, 2, TH, FR, C), BF16),
            pltpu.VMEM((2, 4, 1, FR, C), BF16),
            pltpu.VMEM((2, 2, FR * TW, C), F32),
            pltpu.VMEM((2, 2, FR * (TH + 2), C), F32),
            pltpu.VMEM((inner, C), F32),
            pltpu.VMEM((inner, C), F32),
            pltpu.VMEM((inner, FR, ROWS, C), F32),
            pltpu.VMEM((FR, ROWS, C), F32),
            pltpu.VMEM((FR + 2, 3, XROWS, C), F32),
            pltpu.VMEM((FR + 2, ROWS, K), BF16),
            pltpu.VMEM((2, 2, 48, C), F32),
            pltpu.VMEM((2, 2, 16, C), F32),
            pltpu.VMEM((4, 2, FR, C), F32),
            pltpu.VMEM((inner, 2, 2, 48, C), BF16),
            pltpu.VMEM((inner, 2, 2, 16, C), BF16),
            pltpu.VMEM((inner, 4, 2, FR, C), BF16),
            pltpu.VMEM((LAYERS, 2, ROWS, C), BF16),
            pltpu.VMEM((inner, 2, 2, 48, C), BF16),
            pltpu.VMEM((inner, 2, 2, 16, C), BF16),
            pltpu.VMEM((inner, 4, 2, FR, C), BF16),
            pltpu.VMEM((inner, 2, 48, C), BF16),
            pltpu.VMEM((inner, 2, 16, C), BF16),
            pltpu.VMEM((inner, 4, 2, FR, C), BF16),
            pltpu.VMEM((LAYERS, 2, ROWS, C), BF16),
            pltpu.VMEM((2, 2, 48, C), F32),
            pltpu.VMEM((2, 2, 16, C), F32),
            pltpu.VMEM((4, 2, FR, C), F32),
            pltpu.VMEM((inner, 2, C), F32),
            pltpu.VMEM((inner, n_space - 1, 2, C), F32),
            pltpu.VMEM((inner, n_space, 2, C), F32),
            pltpu.SemaphoreType.DMA((6,)),
            pltpu.SemaphoreType.DMA((LAYERS, 17)),
            pltpu.SemaphoreType.DMA((LAYERS, 17)),
            pltpu.SemaphoreType.DMA((inner, 2)),
            pltpu.SemaphoreType.DMA((inner, 2)),
            pltpu.SemaphoreType.REGULAR,
            pltpu.SemaphoreType.REGULAR,
        ],
        compiler_params=pltpu.CompilerParams(collective_id=0, has_side_effects=True, vmem_limit_bytes=48 << 20),
        cost_estimate=pl.CostEstimate(flops=1274019840, bytes_accessed=2900000, transcendentals=300000),
        name="conv_stack",
    )(*(pltpu.with_memory_space_constraint(value, pltpu.HBM) for value in arguments))
    return result[:, None]


def solution(mesh):
    placed = (P("tm", "space", None, None, None), P(), P(), P())
    return jax.shard_map(
        on_device,
        mesh=mesh,
        in_specs=placed,
        out_specs=P("tm", "space", None, None, None),
        check_vma=False,
    )
```

```python
import jax
import jax.numpy as jnp
from jax import lax
from jax.experimental import pallas as pl
from jax.experimental.pallas import tpu as pltpu
from jax.sharding import PartitionSpec as P

GROUPS = 32
TILE_COLS = 8
BANDS = 4
LAYERS = 3
EPS = 1e-05
F32 = jnp.float32
BF16 = jnp.bfloat16
MESH = pl.DeviceIdType.MESH

FR = 4
TH = 6
TW = 20
C = 128
CELLS = TH * TW
ROWS = 128
PAD = 8
XROWS = PAD + (TH + 2) * TW + 8
K = 9 * C
COUNT = BANDS * TH * TILE_COLS * TW * (C // GROUPS)


def dot(left, right):
    return jnp.dot(left, right, preferred_element_type=F32)


def roll(value, steps):
    return value if steps == 0 else pltpu.roll(value, steps % C, 1)


def pack_sums(total):
    lane = lax.broadcasted_iota(jnp.int32, (1, C), 1) % 4
    moved = {d: roll(total, d) for d in range(-3, 4)}
    first = jnp.zeros((1, C), F32)
    second = jnp.zeros((1, C), F32)
    for f in range(FR):
        group = (moved[f - 3] + moved[f - 2]) + (moved[f - 1] + moved[f])
        first = jnp.where(lane == f, group[f : f + 1], first)
        second = jnp.where(lane == f, group[4 + f : 5 + f], second)
    return jnp.concatenate([first, second], axis=0)


def unpack_sums(packed):
    lane = lax.broadcasted_iota(jnp.int32, (8, C), 1) % 4
    row = lax.broadcasted_iota(jnp.int32, (8, C), 0)
    spread = jnp.where(row < 4, packed[0:1], packed[1:2])
    gap = lane - row % 4
    result = spread
    for d in (-3, -2, -1, 1, 2, 3):
        result = jnp.where(gap == d, roll(spread, d), result)
    return result


def moments(packed, gain):
    sums = unpack_sums(packed) * (1.0 / COUNT)
    mean = sums[0:4]
    var = sums[4:8] - mean * mean
    return mean, lax.rsqrt(var + EPS) * gain


def side(column_part, top_corner, bottom_corner):
    row = lax.broadcasted_iota(jnp.int32, (8, C), 0)
    return jnp.where(row == 0, top_corner, jnp.where(row == TH + 1, bottom_corner, column_part))


FAR_FIRST = sorted(
    ((b, c) for b in range(-1, 3) for c in range(-3, 5) if (b, c) != (0, 0)), key=lambda o: (-abs(o[0]) - abs(o[1]), o)
)

STEPS = ((1, 0), (-1, 0), (0, 1), (0, -1), (-1, -1), (-1, 1), (1, -1), (1, 1))
CORNERS = ((0, 0), (0, TW - 1), (TH - 1, 0), (TH - 1, TW - 1))


def kernel(
    video,
    weights,
    gain_in,
    bias_in,
    out,
    w,
    vid,
    inter,
    first_row,
    first_col,
    first_corner,
    row_cells,
    col_cells,
    gains,
    biases,
    y,
    acc,
    xc,
    im,
    stage_row,
    stage_col,
    stage_corner,
    out_row,
    out_col,
    out_corner,
    out_halo,
    in_row,
    in_col,
    in_corner,
    next_row,
    next_col,
    next_corner,
    halo,
    rim_row,
    rim_col,
    rim_corner,
    packed,
    slots,
    prev_slots,
    load_sem,
    send_sem,
    recv_sem,
    stat_send,
    stat_recv,
    near_sem,
    ready_sem,
):
    tm = lax.axis_index("tm")
    space = lax.axis_index("space")
    n_tm = lax.axis_size("tm")
    n_space = lax.axis_size("space")
    band = space // TILE_COLS
    column = lax.rem(space, TILE_COLS)
    after = lax.rem(tm + 1, n_tm)
    before = lax.rem(tm + n_tm - 1, n_tm)

    bands = {b: lax.rem(band + b + BANDS, BANDS) * TILE_COLS for b in range(-1, 3)}
    columns = {c: lax.rem(column + c + TILE_COLS, TILE_COLS) for c in range(-3, 5)}
    tiles = {(b, c): bands[b] + columns[c] for b in bands for c in columns}

    def tile(b, c):
        return tiles[b, c]

    barrier = pltpu.get_barrier_semaphore()
    has_before = has_after = True

    @pl.when(has_before)
    def _():
        for step in STEPS[::-1] + ((0, 0),):
            pl.semaphore_signal(barrier, inc=1, device_id=(before, tile(*step)), device_id_type=MESH)

    for step in STEPS[::-1]:
        pl.semaphore_signal(barrier, inc=1, device_id=(tm, tile(*step)), device_id_type=MESH)

    loads = [pltpu.make_async_copy(video, vid, load_sem.at[0])]
    for layer in range(LAYERS):
        loads.append(pltpu.make_async_copy(weights.at[layer], w.at[layer], load_sem.at[1 + layer]))
    loads.append(pltpu.make_async_copy(gain_in, gains, load_sem.at[4]))
    loads.append(pltpu.make_async_copy(bias_in, biases, load_sem.at[5]))
    for copy in loads:
        copy.start()
    loads[0].wait()
    inter[...] = vid[...].astype(F32).reshape(FR * CELLS, C)
    for f in range(2):
        whole = jnp.concatenate([inter[pl.ds(2 + f, CELLS, stride=FR), :], jnp.zeros((ROWS - CELLS, C), F32)], axis=0)
        out_halo[0, f] = whole.astype(BF16)
    pl.semaphore_wait(barrier, 2 * len(STEPS) + 1)

    sent = {}

    def send(t, k, source, target, device):
        copy = pltpu.make_async_remote_copy(
            src_ref=source,
            dst_ref=target,
            send_sem=send_sem.at[t, k],
            recv_sem=recv_sem.at[t, k],
            device_id=device,
            device_id_type=MESH,
        )
        copy.start()
        sent[t, k] = copy

    def fill(slot, own, top, bottom, left_side, right_side):
        for c in range(3):
            off = PAD + 1 - c
            xc[slot, c, off : off + TW, :] = top
            xc[slot, c, off + TW : off + TW + CELLS, :] = own
            xc[slot, c, off + TW + CELLS : off + 2 * TW + CELLS, :] = bottom
        xc[slot, 0, pl.ds(PAD, TH + 2, stride=TW), :] = left_side
        xc[slot, 2, pl.ds(PAD + TW - 1, TH + 2, stride=TW), :] = right_side
        zeros = jnp.zeros((ROWS - CELLS, C), F32)
        for b in range(3):
            for c in range(3):
                start = PAD + b * TW
                part = jnp.concatenate([xc[slot, c, start : start + CELLS, :], zeros], axis=0)
                tap = b * 3 + c
                im[slot, :, tap * C : (tap + 1) * C] = part.astype(BF16)

    row8 = lax.broadcasted_iota(jnp.int32, (8, C), 0)
    keep_rows = ((row8 > 0) | (band > 0)) & ((row8 < TH + 1) | (band < BANDS - 1))
    keep_left = keep_rows & (column > 0)
    keep_right = keep_rows & (column < TILE_COLS - 1)

    def frame(slot, parts, act, keep):
        own, top, bottom, left_side, right_side = (act(*part) for part in parts)
        fill(
            slot,
            keep(own),
            keep(jnp.where(band > 0, top, 0.0)),
            keep(jnp.where(band < BANDS - 1, bottom, 0.0)),
            keep(jnp.where(keep_left, left_side, 0.0)),
            keep(jnp.where(keep_right, right_side, 0.0)),
        )

    def same(value, shift=None):
        return value

    def later(value):
        return jnp.where(tm > 0, value, 0.0)

    def split(g, f):
        return (
            (row_cells[g, 0, pl.ds(f, TW, stride=FR), :], None),
            (row_cells[g, 1, pl.ds(f, TW, stride=FR), :], None),
            (col_cells[g, 0, pl.ds(f, TH + 2, stride=FR), :], None),
            (col_cells[g, 1, pl.ds(f, TH + 2, stride=FR), :], None),
        )

    def unpack_rims(g):
        for i in range(2):
            row_cells[g, i] = first_row[g, i].astype(F32).reshape(FR * TW, C)
            col_cells[g, i, FR : FR * (TH + 1), :] = first_col[g, i].astype(F32).reshape(FR * TH, C)
            col_cells[g, i, 0:FR, :] = first_corner[g, i].astype(F32).reshape(FR, C)
            col_cells[g, i, FR * (TH + 1) :, :] = first_corner[g, 2 + i].astype(F32).reshape(FR, C)

    def rims_of(p, f):
        lo = f * TW
        own = 2 * p + f
        rims = [(rim_row[i, p, lo : lo + TW, :], rim_row[i, p, 2 * TW + f : 2 * TW + f + 1, :]) for i in range(2)]
        for i in range(2):
            part = rim_col[i, p, 8 * f : 8 * f + 8, :]
            upper, lower = ((rim_corner[k, 0, own : own + 1, :], rim_corner[k, 1, own : own + 1, :]) for k in (i, 2 + i))
            rims.append((side(part, upper[0], lower[0]), side(part[0:1], upper[1], lower[1])))
        return rims

    for t in range(LAYERS):
        s = t - 1
        if t == 0:
            rims = [vid.at[TH - 1], vid.at[0], vid.at[:, TW - 1], vid.at[:, 0]] + [vid.at[h, pl.ds(c, 1)] for h, c in CORNERS]

            def give(g, where_to, rims=rims):
                lands = [first_row.at[g, 0], first_row.at[g, 1], first_col.at[g, 0], first_col.at[g, 1]] + [
                    first_corner.at[g, 3 - k] for k in range(4)
                ]
                for k in range(7, -1, -1):
                    send(0, 9 * g + k, rims[k], lands[k], (where_to, tile(*STEPS[k])))

            give(0, tm)

            @pl.when(has_after)
            def _(give=give):
                send(0, 8, out_halo.at[0], halo.at[0], (after, space))
                give(1, after)

        else:
            value = y[s]
            sums = [jnp.sum(value[f], axis=0, keepdims=True) for f in range(FR)]
            squares = [jnp.sum(value[f] * value[f], axis=0, keepdims=True) for f in range(FR)]
            packed[s] = pack_sums(jnp.concatenate(sums + squares, axis=0))

            def tell(k, offset, device, buffer, mine, s=s):
                pltpu.make_async_remote_copy(
                    src_ref=packed.at[s],
                    dst_ref=buffer.at[s, k],
                    send_sem=stat_send.at[s, mine],
                    recv_sem=stat_recv.at[s, mine],
                    device_id=(device, tile(*offset)),
                    device_id_type=MESH,
                ).start()

            for k, offset in enumerate(FAR_FIRST):
                tell(k, offset, tm, slots, 0)

            @pl.when(has_after)
            def _(tell=tell, t=t):
                if t == 1:
                    pl.semaphore_wait(ready_sem, 1)
                for k, offset in enumerate(FAR_FIRST + [(0, 0)]):
                    tell(k, offset, after, prev_slots, 1)

            for f in range(FR):
                off = (sums[f] * (1.0 / CELLS)).astype(BF16).astype(F32)
                p, lo = f // 2, f % 2
                for i, first in enumerate((CELLS - TW, 0)):
                    stage_row[i, p, lo * TW : (lo + 1) * TW, :] = y[s, f, first : first + TW, :] - off
                    stage_row[i, p, 2 * TW + lo : 2 * TW + lo + 1, :] = off
                for i, first in enumerate((TW - 1, 0)):
                    stage_col[i, p, 8 * lo : 8 * lo + 8, :] = jnp.broadcast_to(off, (8, C))
                    stage_col[i, p, 8 * lo + 1 : 8 * lo + 1 + TH, :] = y[s, f, pl.ds(first, TH, stride=TW), :] - off
                for k, (h, c) in enumerate(CORNERS):
                    cell = h * TW + c
                    stage_corner[k, 0, f : f + 1, :] = y[s, f, cell : cell + 1, :] - off
                    stage_corner[k, 1, f : f + 1, :] = off
                if p == 1:
                    whole = jnp.concatenate([y[s, f, 0:CELLS, :] - off, jnp.broadcast_to(off, (ROWS - CELLS, C))], axis=0)
                    out_halo[t, lo] = whole.astype(BF16)
            out_row[s] = stage_row[...].astype(BF16)
            out_col[s] = stage_col[...].astype(BF16)
            out_corner[s] = stage_corner[...].astype(BF16)
            for k in range(7, -1, -1):
                if k < 2:
                    source, land = out_row.at[s, k], in_row.at[s, k]
                elif k < 4:
                    source, land = out_col.at[s, k - 2], in_col.at[s, k - 2]
                else:
                    source, land = out_corner.at[s, k - 4], in_corner.at[s, 7 - k]
                send(t, k, source, land, (tm, tile(*STEPS[k])))

            @pl.when(has_after)
            def _(s=s, t=t):
                send(t, 8, out_halo.at[t], halo.at[t], (after, space))
                for k in range(7, -1, -1):
                    if k < 2:
                        source, land = out_row.at[s, k, 1], next_row.at[s, k]
                    elif k < 4:
                        source, land = out_col.at[s, k - 2, 1], next_col.at[s, k - 2]
                    else:
                        source, land = out_corner.at[s, k - 4], next_corner.at[s, 7 - k]
                    send(t, 9 + k, source, land, (after, tile(*STEPS[k])))

        for k in range(8):
            sent[t, k].wait_recv()
        loads[1 + t].wait()

        if t == 0:
            for step in ((0, 2), (0, -2)):
                pl.semaphore_signal(near_sem, inc=1, device_id=(tm, tile(*step)), device_id_type=MESH)
            unpack_rims(0)
            for f in range(FR):
                frame(2 + f, [(inter[pl.ds(f, CELLS, stride=FR), :], None), *split(0, f)], same, same)
        else:
            if t == 1:
                loads[4].wait()
                loads[5].wait()
            gain = gains[s : s + 1, :]
            bias = biases[s : s + 1, :]

            def act_of(f, stats, bias=bias):
                mean, scale = stats

                def act(value, off=0.0):
                    v = (value + (off - mean[f : f + 1])) * scale[f : f + 1] + bias
                    return v / (1.0 + jnp.exp(-v))

                return act

            rim_row[...] = in_row[s].astype(F32)
            rim_col[...] = in_col[s].astype(F32)
            rim_corner[...] = in_corner[s].astype(F32)
            pltpu.make_async_copy(slots.at[s], slots.at[s], stat_recv.at[s, 0]).wait()
            stats = moments(packed[s] + jnp.sum(slots[s], axis=0), gain)
            for f in range(FR):
                frame(2 + f, [(y[s, f, 0:CELLS, :],), *rims_of(f // 2, f % 2)], act_of(f, stats), same)

        w21 = jnp.concatenate([w[t, 2], w[t, 1]], axis=1)
        two = dot(im[2:5].reshape(3 * ROWS, K), w21).reshape(3, ROWS, 2 * C)
        one = dot(im[5], w[t, 2])
        old = dot(im[2:4].reshape(2 * ROWS, K), w[t, 0]).reshape(2, ROWS, C)
        acc[0] = two[0, :, :C]
        acc[1] = two[0, :, C:] + two[1, :, :C]
        acc[2] = two[1, :, C:] + two[2, :, :C] + old[0]
        acc[3] = two[2, :, C:] + one + old[1]

        if t == 0:
            pl.semaphore_wait(near_sem, 2)

        @pl.when(has_before)
        def _(s=s, t=t):
            for k in range(8, 17):
                sent[t, k].wait_recv()
            if t == 0:
                pl.semaphore_signal(ready_sem, inc=1, device_id=(before, space), device_id_type=MESH)
            else:
                pltpu.make_async_copy(prev_slots.at[s], prev_slots.at[s], stat_recv.at[s, 1]).wait()

        if t == 0:
            unpack_rims(1)
            for f in range(2):
                frame(f, [(halo[0, f].astype(F32)[0:CELLS],), *split(1, 2 + f)], same, later)
        else:
            for i in range(2):
                rim_row[i, 1] = next_row[s, i].astype(F32)
                rim_col[i, 1] = next_col[s, i].astype(F32)
            rim_corner[...] = next_corner[s].astype(F32)
            stats = moments(jnp.sum(prev_slots[s], axis=0), gain)
            for f in range(2):
                whole = halo[t, f].astype(F32)
                frame(f, [(whole[0:CELLS], whole[CELLS : CELLS + 1]), *rims_of(1, f)], act_of(2 + f, stats), later)
        w10 = jnp.concatenate([w[t, 1], w[t, 0]], axis=1)
        near = dot(im[1], w10)
        far = dot(im[0], w[t, 0])
        result = [acc[0] + near[:, :C] + far, acc[1] + near[:, C:], acc[2], acc[3]]
        for f in range(FR):
            if t < LAYERS - 1:
                y[t, f] = result[f]
            else:
                for h in range(TH):
                    out[f, h] = result[f][h * TW : (h + 1) * TW].astype(BF16)

    for t in range(LAYERS):
        for k in range(8):
            sent[t, k].wait_send()
    for s in range(LAYERS - 1):
        pltpu.make_async_copy(slots.at[s], slots.at[s], stat_send.at[s, 0]).wait()

    @pl.when(has_after)
    def _():
        for t in range(LAYERS):
            for k in range(8, 17):
                sent[t, k].wait_send()
        for s in range(LAYERS - 1):
            pltpu.make_async_copy(prev_slots.at[s], prev_slots.at[s], stat_send.at[s, 1]).wait()


def on_device(video, conv_weight, norm_gain, norm_bias):
    n_space = lax.axis_size("space")
    inner = LAYERS - 1
    arguments = (
        video.reshape(FR, TH, TW, C).transpose(1, 2, 0, 3),
        conv_weight.reshape(LAYERS, 3, K, C),
        norm_gain,
        norm_bias,
    )
    result = pl.pallas_call(
        kernel,
        out_shape=jax.ShapeDtypeStruct((FR, TH, TW, C), BF16),
        in_specs=[pl.BlockSpec(memory_space=pltpu.HBM)] * 4,
        out_specs=pl.BlockSpec(memory_space=pltpu.VMEM),
        scratch_shapes=[
            pltpu.VMEM((LAYERS, 3, K, C), BF16),
            pltpu.VMEM((TH, TW, FR, C), BF16),
            pltpu.VMEM((FR * CELLS, C), F32),
            pltpu.VMEM((2, 2, TW, FR, C), BF16),
            pltpu.VMEM((2, 2, TH, FR, C), BF16),
            pltpu.VMEM((2, 4, 1, FR, C), BF16),
            pltpu.VMEM((2, 2, FR * TW, C), F32),
            pltpu.VMEM((2, 2, FR * (TH + 2), C), F32),
            pltpu.VMEM((inner, C), F32),
            pltpu.VMEM((inner, C), F32),
            pltpu.VMEM((inner, FR, ROWS, C), F32),
            pltpu.VMEM((FR, ROWS, C), F32),
            pltpu.VMEM((FR + 2, 3, XROWS, C), F32),
            pltpu.VMEM((FR + 2, ROWS, K), BF16),
            pltpu.VMEM((2, 2, 48, C), F32),
            pltpu.VMEM((2, 2, 16, C), F32),
            pltpu.VMEM((4, 2, FR, C), F32),
            pltpu.VMEM((inner, 2, 2, 48, C), BF16),
            pltpu.VMEM((inner, 2, 2, 16, C), BF16),
            pltpu.VMEM((inner, 4, 2, FR, C), BF16),
            pltpu.VMEM((LAYERS, 2, ROWS, C), BF16),
            pltpu.VMEM((inner, 2, 2, 48, C), BF16),
            pltpu.VMEM((inner, 2, 2, 16, C), BF16),
            pltpu.VMEM((inner, 4, 2, FR, C), BF16),
            pltpu.VMEM((inner, 2, 48, C), BF16),
            pltpu.VMEM((inner, 2, 16, C), BF16),
            pltpu.VMEM((inner, 4, 2, FR, C), BF16),
            pltpu.VMEM((LAYERS, 2, ROWS, C), BF16),
            pltpu.VMEM((2, 2, 48, C), F32),
            pltpu.VMEM((2, 2, 16, C), F32),
            pltpu.VMEM((4, 2, FR, C), F32),
            pltpu.VMEM((inner, 2, C), F32),
            pltpu.VMEM((inner, n_space - 1, 2, C), F32),
            pltpu.VMEM((inner, n_space, 2, C), F32),
            pltpu.SemaphoreType.DMA((6,)),
            pltpu.SemaphoreType.DMA((LAYERS, 17)),
            pltpu.SemaphoreType.DMA((LAYERS, 17)),
            pltpu.SemaphoreType.DMA((inner, 2)),
            pltpu.SemaphoreType.DMA((inner, 2)),
            pltpu.SemaphoreType.REGULAR,
            pltpu.SemaphoreType.REGULAR,
        ],
        compiler_params=pltpu.CompilerParams(collective_id=0, has_side_effects=True, vmem_limit_bytes=48 << 20),
        cost_estimate=pl.CostEstimate(flops=1274019840, bytes_accessed=2900000, transcendentals=300000),
        name="conv_stack",
    )(*(pltpu.with_memory_space_constraint(value, pltpu.HBM) for value in arguments))
    return result[:, None]


def solution(mesh):
    placed = (P("tm", "space", None, None, None), P(), P(), P())
    return jax.shard_map(
        on_device,
        mesh=mesh,
        in_specs=placed,
        out_specs=P("tm", "space", None, None, None),
        check_vma=False,
    )
```

```python
import jax
import jax.numpy as jnp
from jax import lax
from jax.experimental import pallas as pl
from jax.experimental.pallas import tpu as pltpu
from jax.sharding import PartitionSpec as P

GROUPS = 32
TILE_COLS = 8
BANDS = 4
LAYERS = 3
EPS = 1e-05
F32 = jnp.float32
BF16 = jnp.bfloat16
MESH = pl.DeviceIdType.MESH

FR = 4
TH = 6
TW = 20
C = 128
CELLS = TH * TW
ROWS = 128
PAD = 8
XROWS = PAD + (TH + 2) * TW + 8
K = 9 * C
COUNT = BANDS * TH * TILE_COLS * TW * (C // GROUPS)


def dot(left, right):
    return jnp.dot(left, right, preferred_element_type=F32)


def roll(value, steps):
    return value if steps == 0 else pltpu.roll(value, steps % C, 1)


def pack_sums(total):
    lane = lax.broadcasted_iota(jnp.int32, (1, C), 1) % 4
    moved = {d: roll(total, d) for d in range(-3, 4)}
    first = jnp.zeros((1, C), F32)
    second = jnp.zeros((1, C), F32)
    for f in range(FR):
        group = (moved[f - 3] + moved[f - 2]) + (moved[f - 1] + moved[f])
        first = jnp.where(lane == f, group[f : f + 1], first)
        second = jnp.where(lane == f, group[4 + f : 5 + f], second)
    return jnp.concatenate([first, second], axis=0)


def unpack_sums(packed):
    lane = lax.broadcasted_iota(jnp.int32, (8, C), 1) % 4
    row = lax.broadcasted_iota(jnp.int32, (8, C), 0)
    spread = jnp.where(row < 4, packed[0:1], packed[1:2])
    gap = lane - row % 4
    result = spread
    for d in (-3, -2, -1, 1, 2, 3):
        result = jnp.where(gap == d, roll(spread, d), result)
    return result


def moments(packed, gain):
    sums = unpack_sums(packed) * (1.0 / COUNT)
    mean = sums[0:4]
    var = sums[4:8] - mean * mean
    return mean, lax.rsqrt(var + EPS) * gain


def side(column_part, top_corner, bottom_corner):
    row = lax.broadcasted_iota(jnp.int32, (8, C), 0)
    return jnp.where(row == 0, top_corner, jnp.where(row == TH + 1, bottom_corner, column_part))


FAR_FIRST = sorted(
    ((b, c) for b in range(-1, 3) for c in range(-3, 5) if (b, c) != (0, 0)), key=lambda o: (-abs(o[0]) - abs(o[1]), o)
)

STEPS = ((1, 0), (-1, 0), (0, 1), (0, -1), (-1, -1), (-1, 1), (1, -1), (1, 1))
CORNERS = ((0, 0), (0, TW - 1), (TH - 1, 0), (TH - 1, TW - 1))


def kernel(
    video,
    weights,
    gain_in,
    bias_in,
    out,
    w,
    vid,
    inter,
    first_row,
    first_col,
    first_corner,
    row_cells,
    col_cells,
    gains,
    biases,
    y,
    acc,
    xc,
    im,
    stage_row,
    stage_col,
    stage_corner,
    out_row,
    out_col,
    out_corner,
    out_halo,
    in_row,
    in_col,
    in_corner,
    next_row,
    next_col,
    next_corner,
    halo,
    rim_row,
    rim_col,
    rim_corner,
    packed,
    slots,
    prev_slots,
    load_sem,
    send_sem,
    recv_sem,
    stat_send,
    stat_recv,
    near_sem,
    ready_sem,
):
    tm = lax.axis_index("tm")
    space = lax.axis_index("space")
    n_tm = lax.axis_size("tm")
    n_space = lax.axis_size("space")
    band = space // TILE_COLS
    column = lax.rem(space, TILE_COLS)
    after = lax.rem(tm + 1, n_tm)
    before = lax.rem(tm + n_tm - 1, n_tm)

    bands = {b: lax.rem(band + b + BANDS, BANDS) * TILE_COLS for b in range(-1, 3)}
    columns = {c: lax.rem(column + c + TILE_COLS, TILE_COLS) for c in range(-3, 5)}
    tiles = {(b, c): bands[b] + columns[c] for b in bands for c in columns}

    def tile(b, c):
        return tiles[b, c]

    barrier = pltpu.get_barrier_semaphore()
    has_before = tm > 0
    has_after = tm < n_tm - 1

    @pl.when(has_before)
    def _():
        for step in STEPS[::-1] + ((0, 0),):
            pl.semaphore_signal(barrier, inc=1, device_id=(before, tile(*step)), device_id_type=MESH)

    for step in STEPS[::-1]:
        pl.semaphore_signal(barrier, inc=1, device_id=(tm, tile(*step)), device_id_type=MESH)

    loads = [pltpu.make_async_copy(video, vid, load_sem.at[0])]
    for layer in range(LAYERS):
        loads.append(pltpu.make_async_copy(weights.at[layer], w.at[layer], load_sem.at[1 + layer]))
    loads.append(pltpu.make_async_copy(gain_in, gains, load_sem.at[4]))
    loads.append(pltpu.make_async_copy(bias_in, biases, load_sem.at[5]))
    for copy in loads:
        copy.start()
    loads[0].wait()
    inter[...] = vid[...].astype(F32).reshape(FR * CELLS, C)
    for f in range(2):
        whole = jnp.concatenate([inter[pl.ds(2 + f, CELLS, stride=FR), :], jnp.zeros((ROWS - CELLS, C), F32)], axis=0)
        out_halo[0, f] = whole.astype(BF16)
    pl.semaphore_wait(barrier, len(STEPS) + jnp.where(has_after, len(STEPS) + 1, 0))

    def ends(t, k):
        if k == 8:
            return out_halo.at[t], halo.at[t]
        g, k = divmod(k, 9)
        s = t - 1
        if t == 0:
            if k < 2:
                return vid.at[(TH - 1, 0)[k]], first_row.at[g, k]
            if k < 4:
                return vid.at[:, (TW - 1, 0)[k - 2]], first_col.at[g, k - 2]
            h, c = CORNERS[k - 4]
            return vid.at[h, pl.ds(c, 1)], first_corner.at[g, 7 - k]
        if k < 2:
            return (out_row.at[s, k, 1], next_row.at[s, k]) if g else (out_row.at[s, k], in_row.at[s, k])
        if k < 4:
            k = k - 2
            return (out_col.at[s, k, 1], next_col.at[s, k]) if g else (out_col.at[s, k], in_col.at[s, k])
        return out_corner.at[s, k - 4], (next_corner if g else in_corner).at[s, 7 - k]

    def message(t, k):
        source, land = ends(t, k)
        step = (0, 0) if k == 8 else STEPS[k % 9]
        return pltpu.make_async_remote_copy(
            src_ref=source,
            dst_ref=land,
            send_sem=send_sem.at[t, k],
            recv_sem=recv_sem.at[t, k],
            device_id=(tm if k < 8 else after, tile(*step)),
            device_id_type=MESH,
        )

    def send_all(t):
        for k in range(7, -1, -1):
            message(t, k).start()

        @pl.when(has_after)
        def _():
            for k in (8, 16, 15, 14, 13, 12, 11, 10, 9):
                message(t, k).start()

    def fill(slot, own, top, bottom, left_side, right_side):
        for c in range(3):
            off = PAD + 1 - c
            xc[slot, c, off : off + TW, :] = top
            xc[slot, c, off + TW : off + TW + CELLS, :] = own
            xc[slot, c, off + TW + CELLS : off + 2 * TW + CELLS, :] = bottom
        xc[slot, 0, pl.ds(PAD, TH + 2, stride=TW), :] = left_side
        xc[slot, 2, pl.ds(PAD + TW - 1, TH + 2, stride=TW), :] = right_side
        zeros = jnp.zeros((ROWS - CELLS, C), F32)
        for b in range(3):
            for c in range(3):
                start = PAD + b * TW
                part = jnp.concatenate([xc[slot, c, start : start + CELLS, :], zeros], axis=0)
                tap = b * 3 + c
                im[slot, :, tap * C : (tap + 1) * C] = part.astype(BF16)

    row8 = lax.broadcasted_iota(jnp.int32, (8, C), 0)
    keep_rows = ((row8 > 0) | (band > 0)) & ((row8 < TH + 1) | (band < BANDS - 1))
    keep_left = keep_rows & (column > 0)
    keep_right = keep_rows & (column < TILE_COLS - 1)

    def frame(slot, parts, act, keep):
        own, top, bottom, left_side, right_side = (act(*part) for part in parts)
        fill(
            slot,
            keep(own),
            keep(jnp.where(band > 0, top, 0.0)),
            keep(jnp.where(band < BANDS - 1, bottom, 0.0)),
            keep(jnp.where(keep_left, left_side, 0.0)),
            keep(jnp.where(keep_right, right_side, 0.0)),
        )

    def same(value, shift=None):
        return value

    def later(value):
        return jnp.where(tm > 0, value, 0.0)

    def split(g, f):
        return (
            (row_cells[g, 0, pl.ds(f, TW, stride=FR), :], None),
            (row_cells[g, 1, pl.ds(f, TW, stride=FR), :], None),
            (col_cells[g, 0, pl.ds(f, TH + 2, stride=FR), :], None),
            (col_cells[g, 1, pl.ds(f, TH + 2, stride=FR), :], None),
        )

    def unpack_rims(g):
        for i in range(2):
            row_cells[g, i] = first_row[g, i].astype(F32).reshape(FR * TW, C)
            col_cells[g, i, FR : FR * (TH + 1), :] = first_col[g, i].astype(F32).reshape(FR * TH, C)
            col_cells[g, i, 0:FR, :] = first_corner[g, i].astype(F32).reshape(FR, C)
            col_cells[g, i, FR * (TH + 1) :, :] = first_corner[g, 2 + i].astype(F32).reshape(FR, C)

    def rims_of(p, f):
        lo = f * TW
        own = 2 * p + f
        rims = [(rim_row[i, p, lo : lo + TW, :], rim_row[i, p, 2 * TW + f : 2 * TW + f + 1, :]) for i in range(2)]
        for i in range(2):
            part = rim_col[i, p, 8 * f : 8 * f + 8, :]
            upper, lower = ((rim_corner[k, 0, own : own + 1, :], rim_corner[k, 1, own : own + 1, :]) for k in (i, 2 + i))
            rims.append((side(part, upper[0], lower[0]), side(part[0:1], upper[1], lower[1])))
        return rims

    for t in range(LAYERS):
        s = t - 1
        if t == 0:
            send_all(0)
        else:
            value = y[s]
            sums = [jnp.sum(value[f], axis=0, keepdims=True) for f in range(FR)]
            squares = [jnp.sum(value[f] * value[f], axis=0, keepdims=True) for f in range(FR)]
            packed[s] = pack_sums(jnp.concatenate(sums + squares, axis=0))

            def tell(k, offset, device, buffer, mine, s=s):
                pltpu.make_async_remote_copy(
                    src_ref=packed.at[s],
                    dst_ref=buffer.at[s, k],
                    send_sem=stat_send.at[s, mine],
                    recv_sem=stat_recv.at[s, mine],
                    device_id=(device, tile(*offset)),
                    device_id_type=MESH,
                ).start()

            for k, offset in enumerate(FAR_FIRST):
                tell(k, offset, tm, slots, 0)

            @pl.when(has_after)
            def _(tell=tell, t=t):
                if t == 1:
                    pl.semaphore_wait(ready_sem, 1)
                for k, offset in enumerate(FAR_FIRST + [(0, 0)]):
                    tell(k, offset, after, prev_slots, 1)

            for f in range(FR):
                off = (sums[f] * (1.0 / CELLS)).astype(BF16).astype(F32)
                p, lo = f // 2, f % 2
                for i, first in enumerate((CELLS - TW, 0)):
                    stage_row[i, p, lo * TW : (lo + 1) * TW, :] = y[s, f, first : first + TW, :] - off
                    stage_row[i, p, 2 * TW + lo : 2 * TW + lo + 1, :] = off
                for i, first in enumerate((TW - 1, 0)):
                    stage_col[i, p, 8 * lo : 8 * lo + 8, :] = jnp.broadcast_to(off, (8, C))
                    stage_col[i, p, 8 * lo + 1 : 8 * lo + 1 + TH, :] = y[s, f, pl.ds(first, TH, stride=TW), :] - off
                for k, (h, c) in enumerate(CORNERS):
                    cell = h * TW + c
                    stage_corner[k, 0, f : f + 1, :] = y[s, f, cell : cell + 1, :] - off
                    stage_corner[k, 1, f : f + 1, :] = off
                if p == 1:
                    whole = jnp.concatenate([y[s, f, 0:CELLS, :] - off, jnp.broadcast_to(off, (ROWS - CELLS, C))], axis=0)
                    out_halo[t, lo] = whole.astype(BF16)
            out_row[s] = stage_row[...].astype(BF16)
            out_col[s] = stage_col[...].astype(BF16)
            out_corner[s] = stage_corner[...].astype(BF16)
            send_all(t)

        for k in range(8):
            message(t, k).wait_recv()
        loads[1 + t].wait()

        if t == 0:
            for step in ((0, 2), (0, -2)):
                pl.semaphore_signal(near_sem, inc=1, device_id=(tm, tile(*step)), device_id_type=MESH)
            unpack_rims(0)
            for f in range(FR):
                frame(2 + f, [(inter[pl.ds(f, CELLS, stride=FR), :], None), *split(0, f)], same, same)
        else:
            if t == 1:
                loads[4].wait()
                loads[5].wait()
            gain = gains[s : s + 1, :]
            bias = biases[s : s + 1, :]

            def act_of(f, stats, bias=bias):
                mean, scale = stats

                def act(value, off=0.0):
                    v = (value + (off - mean[f : f + 1])) * scale[f : f + 1] + bias
                    return v / (1.0 + jnp.exp(-v))

                return act

            rim_row[...] = in_row[s].astype(F32)
            rim_col[...] = in_col[s].astype(F32)
            rim_corner[...] = in_corner[s].astype(F32)
            pltpu.make_async_copy(slots.at[s], slots.at[s], stat_recv.at[s, 0]).wait()
            stats = moments(packed[s] + jnp.sum(slots[s], axis=0), gain)
            for f in range(FR):
                frame(2 + f, [(y[s, f, 0:CELLS, :],), *rims_of(f // 2, f % 2)], act_of(f, stats), same)

        w21 = jnp.concatenate([w[t, 2], w[t, 1]], axis=1)
        two = dot(im[2:5].reshape(3 * ROWS, K), w21).reshape(3, ROWS, 2 * C)
        one = dot(im[5], w[t, 2])
        old = dot(im[2:4].reshape(2 * ROWS, K), w[t, 0]).reshape(2, ROWS, C)
        acc[0] = two[0, :, :C]
        acc[1] = two[0, :, C:] + two[1, :, :C]
        acc[2] = two[1, :, C:] + two[2, :, :C] + old[0]
        acc[3] = two[2, :, C:] + one + old[1]

        if t == 0:
            pl.semaphore_wait(near_sem, 2)

        @pl.when(has_before)
        def _(s=s, t=t):
            for k in range(8, 17):
                message(t, k).wait_recv()
            if t == 0:
                pl.semaphore_signal(ready_sem, inc=1, device_id=(before, space), device_id_type=MESH)
            else:
                pltpu.make_async_copy(prev_slots.at[s], prev_slots.at[s], stat_recv.at[s, 1]).wait()

        if t == 0:
            unpack_rims(1)
            for f in range(2):
                frame(f, [(halo[0, f].astype(F32)[0:CELLS],), *split(1, 2 + f)], same, later)
        else:
            for i in range(2):
                rim_row[i, 1] = next_row[s, i].astype(F32)
                rim_col[i, 1] = next_col[s, i].astype(F32)
            rim_corner[...] = next_corner[s].astype(F32)
            stats = moments(jnp.sum(prev_slots[s], axis=0), gain)
            for f in range(2):
                whole = halo[t, f].astype(F32)
                frame(f, [(whole[0:CELLS], whole[CELLS : CELLS + 1]), *rims_of(1, f)], act_of(2 + f, stats), later)
        w10 = jnp.concatenate([w[t, 1], w[t, 0]], axis=1)
        near = dot(im[1], w10)
        far = dot(im[0], w[t, 0])
        result = [acc[0] + near[:, :C] + far, acc[1] + near[:, C:], acc[2], acc[3]]
        for f in range(FR):
            if t < LAYERS - 1:
                y[t, f] = result[f]
            else:
                for h in range(TH):
                    out[f, h] = result[f][h * TW : (h + 1) * TW].astype(BF16)

    for t in range(LAYERS):
        for k in range(8):
            message(t, k).wait_send()
    for s in range(LAYERS - 1):
        pltpu.make_async_copy(slots.at[s], slots.at[s], stat_send.at[s, 0]).wait()

    @pl.when(has_after)
    def _():
        for t in range(LAYERS):
            for k in range(8, 17):
                message(t, k).wait_send()
        for s in range(LAYERS - 1):
            pltpu.make_async_copy(prev_slots.at[s], prev_slots.at[s], stat_send.at[s, 1]).wait()


def on_device(video, conv_weight, norm_gain, norm_bias):
    n_space = lax.axis_size("space")
    inner = LAYERS - 1
    arguments = (
        video.reshape(FR, TH, TW, C).transpose(1, 2, 0, 3),
        conv_weight.reshape(LAYERS, 3, K, C),
        norm_gain,
        norm_bias,
    )
    result = pl.pallas_call(
        kernel,
        out_shape=jax.ShapeDtypeStruct((FR, TH, TW, C), BF16),
        in_specs=[pl.BlockSpec(memory_space=pltpu.HBM)] * 4,
        out_specs=pl.BlockSpec(memory_space=pltpu.VMEM),
        scratch_shapes=[
            pltpu.VMEM((LAYERS, 3, K, C), BF16),
            pltpu.VMEM((TH, TW, FR, C), BF16),
            pltpu.VMEM((FR * CELLS, C), F32),
            pltpu.VMEM((2, 2, TW, FR, C), BF16),
            pltpu.VMEM((2, 2, TH, FR, C), BF16),
            pltpu.VMEM((2, 4, 1, FR, C), BF16),
            pltpu.VMEM((2, 2, FR * TW, C), F32),
            pltpu.VMEM((2, 2, FR * (TH + 2), C), F32),
            pltpu.VMEM((inner, C), F32),
            pltpu.VMEM((inner, C), F32),
            pltpu.VMEM((inner, FR, ROWS, C), F32),
            pltpu.VMEM((FR, ROWS, C), F32),
            pltpu.VMEM((FR + 2, 3, XROWS, C), F32),
            pltpu.VMEM((FR + 2, ROWS, K), BF16),
            pltpu.VMEM((2, 2, 48, C), F32),
            pltpu.VMEM((2, 2, 16, C), F32),
            pltpu.VMEM((4, 2, FR, C), F32),
            pltpu.VMEM((inner, 2, 2, 48, C), BF16),
            pltpu.VMEM((inner, 2, 2, 16, C), BF16),
            pltpu.VMEM((inner, 4, 2, FR, C), BF16),
            pltpu.VMEM((LAYERS, 2, ROWS, C), BF16),
            pltpu.VMEM((inner, 2, 2, 48, C), BF16),
            pltpu.VMEM((inner, 2, 2, 16, C), BF16),
            pltpu.VMEM((inner, 4, 2, FR, C), BF16),
            pltpu.VMEM((inner, 2, 48, C), BF16),
            pltpu.VMEM((inner, 2, 16, C), BF16),
            pltpu.VMEM((inner, 4, 2, FR, C), BF16),
            pltpu.VMEM((LAYERS, 2, ROWS, C), BF16),
            pltpu.VMEM((2, 2, 48, C), F32),
            pltpu.VMEM((2, 2, 16, C), F32),
            pltpu.VMEM((4, 2, FR, C), F32),
            pltpu.VMEM((inner, 2, C), F32),
            pltpu.VMEM((inner, n_space - 1, 2, C), F32),
            pltpu.VMEM((inner, n_space, 2, C), F32),
            pltpu.SemaphoreType.DMA((6,)),
            pltpu.SemaphoreType.DMA((LAYERS, 17)),
            pltpu.SemaphoreType.DMA((LAYERS, 17)),
            pltpu.SemaphoreType.DMA((inner, 2)),
            pltpu.SemaphoreType.DMA((inner, 2)),
            pltpu.SemaphoreType.REGULAR,
            pltpu.SemaphoreType.REGULAR,
        ],
        compiler_params=pltpu.CompilerParams(collective_id=0, has_side_effects=True, vmem_limit_bytes=48 << 20),
        cost_estimate=pl.CostEstimate(flops=1274019840, bytes_accessed=2900000, transcendentals=300000),
        name="conv_stack",
    )(*(pltpu.with_memory_space_constraint(value, pltpu.HBM) for value in arguments))
    return result[:, None]


def solution(mesh):
    placed = (P("tm", "space", None, None, None), P(), P(), P())
    return jax.shard_map(
        on_device,
        mesh=mesh,
        in_specs=placed,
        out_specs=P("tm", "space", None, None, None),
        check_vma=False,
    )
```

```python
import jax
import jax.numpy as jnp
from jax import lax
from jax.experimental import pallas as pl
from jax.experimental.pallas import tpu as pltpu
from jax.sharding import PartitionSpec as P

GROUPS = 32
TILE_COLS = 8
BANDS = 4
LAYERS = 3
EPS = 1e-05
F32 = jnp.float32
BF16 = jnp.bfloat16
MESH = pl.DeviceIdType.MESH

FR = 4
TH = 6
TW = 20
C = 128
CELLS = TH * TW
ROWS = 128
PAD = 8
XROWS = PAD + (TH + 2) * TW + 8
K = 9 * C
COUNT = BANDS * TH * TILE_COLS * TW * (C // GROUPS)


def dot(left, right):
    return jnp.dot(left, right, preferred_element_type=F32)


def roll(value, steps):
    return value if steps == 0 else pltpu.roll(value, steps % C, 1)


def pack_sums(total):
    lane = lax.broadcasted_iota(jnp.int32, (1, C), 1) % 4
    moved = {d: roll(total, d) for d in range(-3, 4)}
    first = jnp.zeros((1, C), F32)
    second = jnp.zeros((1, C), F32)
    for f in range(FR):
        group = (moved[f - 3] + moved[f - 2]) + (moved[f - 1] + moved[f])
        first = jnp.where(lane == f, group[f : f + 1], first)
        second = jnp.where(lane == f, group[4 + f : 5 + f], second)
    return jnp.concatenate([first, second], axis=0)


def unpack_sums(packed):
    lane = lax.broadcasted_iota(jnp.int32, (8, C), 1) % 4
    row = lax.broadcasted_iota(jnp.int32, (8, C), 0)
    spread = jnp.where(row < 4, packed[0:1], packed[1:2])
    gap = lane - row % 4
    result = spread
    for d in (-3, -2, -1, 1, 2, 3):
        result = jnp.where(gap == d, roll(spread, d), result)
    return result


def moments(packed, gain):
    sums = unpack_sums(packed) * (1.0 / COUNT)
    mean = sums[0:4]
    var = sums[4:8] - mean * mean
    return mean, lax.rsqrt(var + EPS) * gain


def side(column_part, top_corner, bottom_corner):
    row = lax.broadcasted_iota(jnp.int32, (8, C), 0)
    return jnp.where(row == 0, top_corner, jnp.where(row == TH + 1, bottom_corner, column_part))


FAR_FIRST = sorted(
    ((b, c) for b in range(-1, 3) for c in range(-3, 5) if (b, c) != (0, 0)), key=lambda o: (-abs(o[0]) - abs(o[1]), o)
)

STEPS = ((1, 0), (-1, 0), (0, 1), (0, -1), (-1, -1), (-1, 1), (1, -1), (1, 1))
CORNERS = ((0, 0), (0, TW - 1), (TH - 1, 0), (TH - 1, TW - 1))


def kernel(
    video,
    weights,
    gain_in,
    bias_in,
    out,
    w,
    vid,
    inter,
    first_row,
    first_col,
    first_corner,
    row_cells,
    col_cells,
    gains,
    biases,
    y,
    acc,
    xc,
    im,
    stage_row,
    stage_col,
    stage_corner,
    out_row,
    out_col,
    out_corner,
    out_halo,
    in_row,
    in_col,
    in_corner,
    next_row,
    next_col,
    next_corner,
    halo,
    rim_row,
    rim_col,
    rim_corner,
    packed,
    slots,
    prev_slots,
    load_sem,
    send_sem,
    recv_sem,
    stat_send,
    stat_recv,
    near_sem,
    ready_sem,
):
    tm = lax.axis_index("tm")
    space = lax.axis_index("space")
    n_tm = lax.axis_size("tm")
    n_space = lax.axis_size("space")
    band = space // TILE_COLS
    column = lax.rem(space, TILE_COLS)
    after = lax.rem(tm + 1, n_tm)
    before = lax.rem(tm + n_tm - 1, n_tm)

    bands = {b: lax.rem(band + b + BANDS, BANDS) * TILE_COLS for b in range(-1, 3)}
    columns = {c: lax.rem(column + c + TILE_COLS, TILE_COLS) for c in range(-3, 5)}
    tiles = {(b, c): bands[b] + columns[c] for b in bands for c in columns}

    def tile(b, c):
        return tiles[b, c]

    barrier = pltpu.get_barrier_semaphore()
    has_before = tm > 0
    has_after = tm < n_tm - 1

    @pl.when(has_before)
    def _():
        for step in STEPS[::-1] + ((0, 0),):
            pl.semaphore_signal(barrier, inc=1, device_id=(before, tile(*step)), device_id_type=MESH)

    for step in STEPS[::-1]:
        pl.semaphore_signal(barrier, inc=1, device_id=(tm, tile(*step)), device_id_type=MESH)

    loads = [pltpu.make_async_copy(video, vid, load_sem.at[0])]
    for layer in range(LAYERS):
        loads.append(pltpu.make_async_copy(weights.at[layer], w.at[layer], load_sem.at[1 + layer]))
    loads.append(pltpu.make_async_copy(gain_in, gains, load_sem.at[4]))
    loads.append(pltpu.make_async_copy(bias_in, biases, load_sem.at[5]))
    for copy in loads:
        copy.start()
    loads[0].wait()
    inter[...] = vid[...].astype(F32).reshape(FR * CELLS, C)
    for f in range(2):
        whole = jnp.concatenate([inter[pl.ds(2 + f, CELLS, stride=FR), :], jnp.zeros((ROWS - CELLS, C), F32)], axis=0)
        out_halo[0, f] = whole.astype(BF16)
    pl.semaphore_wait(barrier, len(STEPS) + jnp.where(has_after, len(STEPS) + 1, 0))

    def ends(t, k):
        if k == 8:
            return out_halo.at[t], halo.at[t]
        g, k = divmod(k, 9)
        s = t - 1
        if t == 0:
            if k < 2:
                return vid.at[(TH - 1, 0)[k]], first_row.at[g, k]
            if k < 4:
                return vid.at[:, (TW - 1, 0)[k - 2]], first_col.at[g, k - 2]
            h, c = CORNERS[k - 4]
            return vid.at[h, pl.ds(c, 1)], first_corner.at[g, 7 - k]
        if k < 2:
            return (out_row.at[s, k, 1], next_row.at[s, k]) if g else (out_row.at[s, k], in_row.at[s, k])
        if k < 4:
            k = k - 2
            return (out_col.at[s, k, 1], next_col.at[s, k]) if g else (out_col.at[s, k], in_col.at[s, k])
        return out_corner.at[s, k - 4], (next_corner if g else in_corner).at[s, 7 - k]

    def message(t, k):
        source, land = ends(t, k)
        step = (0, 0) if k == 8 else STEPS[k % 9]
        return pltpu.make_async_remote_copy(
            src_ref=source,
            dst_ref=land,
            send_sem=send_sem.at[t, k],
            recv_sem=recv_sem.at[t, k],
            device_id=(tm if k < 8 else after, tile(*step)),
            device_id_type=MESH,
        )

    def send_all(t):
        for k in range(7, -1, -1):
            message(t, k).start()

        @pl.when(has_after)
        def _():
            for k in (8, 16, 15, 14, 13, 12, 11, 10, 9):
                message(t, k).start()

    def fill(slot, own, top, bottom, left_side, right_side):
        for c in range(3):
            off = PAD + 1 - c
            xc[slot, c, off : off + TW, :] = top
            xc[slot, c, off + TW : off + TW + CELLS, :] = own
            xc[slot, c, off + TW + CELLS : off + 2 * TW + CELLS, :] = bottom
        xc[slot, 0, pl.ds(PAD, TH + 2, stride=TW), :] = left_side
        xc[slot, 2, pl.ds(PAD + TW - 1, TH + 2, stride=TW), :] = right_side
        zeros = jnp.zeros((ROWS - CELLS, C), F32)
        for b in range(3):
            for c in range(3):
                start = PAD + b * TW
                part = jnp.concatenate([xc[slot, c, start : start + CELLS, :], zeros], axis=0)
                tap = b * 3 + c
                im[slot, :, tap * C : (tap + 1) * C] = part.astype(BF16)

    row8 = lax.broadcasted_iota(jnp.int32, (8, C), 0)
    keep_rows = ((row8 > 0) | (band > 0)) & ((row8 < TH + 1) | (band < BANDS - 1))
    keep_left = keep_rows & (column > 0)
    keep_right = keep_rows & (column < TILE_COLS - 1)

    def frame(slot, parts, act, keep):
        own, top, bottom, left_side, right_side = (act(*part) for part in parts)
        fill(
            slot,
            keep(own),
            keep(jnp.where(band > 0, top, 0.0)),
            keep(jnp.where(band < BANDS - 1, bottom, 0.0)),
            keep(jnp.where(keep_left, left_side, 0.0)),
            keep(jnp.where(keep_right, right_side, 0.0)),
        )

    def same(value, shift=None):
        return value

    def later(value):
        return jnp.where(tm > 0, value, 0.0)

    def split(g, f):
        return (
            (row_cells[g, 0, pl.ds(f, TW, stride=FR), :], None),
            (row_cells[g, 1, pl.ds(f, TW, stride=FR), :], None),
            (col_cells[g, 0, pl.ds(f, TH + 2, stride=FR), :], None),
            (col_cells[g, 1, pl.ds(f, TH + 2, stride=FR), :], None),
        )

    def unpack_rims(g):
        for i in range(2):
            row_cells[g, i] = first_row[g, i].astype(F32).reshape(FR * TW, C)
            col_cells[g, i, FR : FR * (TH + 1), :] = first_col[g, i].astype(F32).reshape(FR * TH, C)
            col_cells[g, i, 0:FR, :] = first_corner[g, i].astype(F32).reshape(FR, C)
            col_cells[g, i, FR * (TH + 1) : FR * (TH + 2), :] = first_corner[g, 2 + i].astype(F32).reshape(FR, C)

    def rims_of(p, f):
        lo = f * TW
        own = 2 * p + f
        rims = [(rim_row[i, p, lo : lo + TW, :], rim_row[i, p, 2 * TW + f : 2 * TW + f + 1, :]) for i in range(2)]
        for i in range(2):
            part = rim_col[i, p, 8 * f : 8 * f + 8, :]
            upper, lower = ((rim_corner[k, 0, own : own + 1, :], rim_corner[k, 1, own : own + 1, :]) for k in (i, 2 + i))
            rims.append((side(part, upper[0], lower[0]), side(part[0:1], upper[1], lower[1])))
        return rims

    for t in range(LAYERS):
        s = t - 1
        if t == 0:
            send_all(0)
        else:
            value = y[s, 0:FR]
            sums = [jnp.sum(value[f], axis=0, keepdims=True) for f in range(FR)]
            squares = [jnp.sum(value[f] * value[f], axis=0, keepdims=True) for f in range(FR)]
            packed[s] = pack_sums(jnp.concatenate(sums + squares, axis=0))

            def tell(k, offset, device, buffer, mine, s=s):
                pltpu.make_async_remote_copy(
                    src_ref=packed.at[s],
                    dst_ref=buffer.at[s, k],
                    send_sem=stat_send.at[s, mine],
                    recv_sem=stat_recv.at[s, mine],
                    device_id=(device, tile(*offset)),
                    device_id_type=MESH,
                ).start()

            for k, offset in enumerate(FAR_FIRST):
                tell(k, offset, tm, slots, 0)

            @pl.when(has_after)
            def _(tell=tell, t=t):
                if t == 1:
                    pl.semaphore_wait(ready_sem, 1)
                for k, offset in enumerate(FAR_FIRST + [(0, 0)]):
                    tell(k, offset, after, prev_slots, 1)

            for f in range(FR):
                off = (sums[f] * (1.0 / CELLS)).astype(BF16).astype(F32)
                p, lo = f // 2, f % 2
                for i, first in enumerate((CELLS - TW, 0)):
                    stage_row[i, p, lo * TW : (lo + 1) * TW, :] = y[s, f, first : first + TW, :] - off
                    stage_row[i, p, 2 * TW + lo : 2 * TW + lo + 1, :] = off
                for i, first in enumerate((TW - 1, 0)):
                    stage_col[i, p, 8 * lo : 8 * lo + 8, :] = jnp.broadcast_to(off, (8, C))
                    stage_col[i, p, 8 * lo + 1 : 8 * lo + 1 + TH, :] = y[s, f, pl.ds(first, TH, stride=TW), :] - off
                for k, (h, c) in enumerate(CORNERS):
                    cell = h * TW + c
                    stage_corner[k, 0, f : f + 1, :] = y[s, f, cell : cell + 1, :] - off
                    stage_corner[k, 1, f : f + 1, :] = off
                if p == 1:
                    whole = jnp.concatenate([y[s, f, 0:CELLS, :] - off, jnp.broadcast_to(off, (ROWS - CELLS, C))], axis=0)
                    out_halo[t, lo] = whole.astype(BF16)
            out_row[s] = stage_row[:, :, 0:48, :].astype(BF16)
            out_col[s] = stage_col[:, :, 0:16, :].astype(BF16)
            out_corner[s] = stage_corner[:, :, 0:FR, :].astype(BF16)
            send_all(t)

        for k in range(8):
            message(t, k).wait_recv()
        loads[1 + t].wait()

        if t == 0:
            for step in ((0, 2), (0, -2)):
                pl.semaphore_signal(near_sem, inc=1, device_id=(tm, tile(*step)), device_id_type=MESH)
            unpack_rims(0)
            for f in range(FR):
                frame(2 + f, [(inter[pl.ds(f, CELLS, stride=FR), :], None), *split(0, f)], same, same)
        else:
            if t == 1:
                loads[4].wait()
                loads[5].wait()
            gain = gains[s : s + 1, :]
            bias = biases[s : s + 1, :]

            def act_of(f, stats, bias=bias):
                mean, scale = stats

                def act(value, off=0.0):
                    v = (value + (off - mean[f : f + 1])) * scale[f : f + 1] + bias
                    return v / (1.0 + jnp.exp(-v))

                return act

            rim_row[:, :, 0:48, :] = in_row[s].astype(F32)
            rim_col[:, :, 0:16, :] = in_col[s].astype(F32)
            rim_corner[:, :, 0:FR, :] = in_corner[s].astype(F32)
            pltpu.make_async_copy(slots.at[s], slots.at[s], stat_recv.at[s, 0]).wait()
            stats = moments(packed[s] + jnp.sum(slots[s], axis=0), gain)
            for f in range(FR):
                frame(2 + f, [(y[s, f, 0:CELLS, :],), *rims_of(f // 2, f % 2)], act_of(f, stats), same)

        w21 = jnp.concatenate([w[t, 2], w[t, 1]], axis=1)
        two = dot(im[2:5].reshape(3 * ROWS, K), w21).reshape(3, ROWS, 2 * C)
        one = dot(im[5], w[t, 2])
        old = dot(im[2:4].reshape(2 * ROWS, K), w[t, 0]).reshape(2, ROWS, C)
        acc[0] = two[0, :, :C]
        acc[1] = two[0, :, C:] + two[1, :, :C]
        acc[2] = two[1, :, C:] + two[2, :, :C] + old[0]
        acc[3] = two[2, :, C:] + one + old[1]

        if t == 0:
            pl.semaphore_wait(near_sem, 2)

        @pl.when(has_before)
        def _(s=s, t=t):
            for k in range(8, 17):
                message(t, k).wait_recv()
            if t == 0:
                pl.semaphore_signal(ready_sem, inc=1, device_id=(before, space), device_id_type=MESH)
            else:
                pltpu.make_async_copy(prev_slots.at[s], prev_slots.at[s], stat_recv.at[s, 1]).wait()

        if t == 0:
            unpack_rims(1)
            for f in range(2):
                frame(f, [(halo[0, f].astype(F32)[0:CELLS],), *split(1, 2 + f)], same, later)
        else:
            for i in range(2):
                rim_row[i, 1, 0:48, :] = next_row[s, i].astype(F32)
                rim_col[i, 1, 0:16, :] = next_col[s, i].astype(F32)
            rim_corner[:, :, 0:FR, :] = next_corner[s].astype(F32)
            stats = moments(jnp.sum(prev_slots[s], axis=0), gain)
            for f in range(2):
                whole = halo[t, f].astype(F32)
                frame(f, [(whole[0:CELLS], whole[CELLS : CELLS + 1]), *rims_of(1, f)], act_of(2 + f, stats), later)
        w10 = jnp.concatenate([w[t, 1], w[t, 0]], axis=1)
        near = dot(im[1], w10)
        far = dot(im[0], w[t, 0])
        result = [acc[0] + near[:, :C] + far, acc[1] + near[:, C:], acc[2], acc[3]]
        for f in range(FR):
            if t < LAYERS - 1:
                y[t, f] = result[f]
            else:
                for h in range(TH):
                    out[f, h] = result[f][h * TW : (h + 1) * TW].astype(BF16)

    for t in range(LAYERS):
        for k in range(8):
            message(t, k).wait_send()
    for s in range(LAYERS - 1):
        pltpu.make_async_copy(slots.at[s], slots.at[s], stat_send.at[s, 0]).wait()

    @pl.when(has_after)
    def _():
        for t in range(LAYERS):
            for k in range(8, 17):
                message(t, k).wait_send()
        for s in range(LAYERS - 1):
            pltpu.make_async_copy(prev_slots.at[s], prev_slots.at[s], stat_send.at[s, 1]).wait()


def on_device(video, conv_weight, norm_gain, norm_bias):
    n_space = lax.axis_size("space")
    inner = LAYERS - 1
    arguments = (
        video.reshape(FR, TH, TW, C).transpose(1, 2, 0, 3),
        conv_weight.reshape(LAYERS, 3, K, C),
        norm_gain,
        norm_bias,
    )
    result = pl.pallas_call(
        kernel,
        out_shape=jax.ShapeDtypeStruct((FR, TH, TW, C), BF16),
        in_specs=[pl.BlockSpec(memory_space=pltpu.HBM)] * 4,
        out_specs=pl.BlockSpec(memory_space=pltpu.VMEM),
        scratch_shapes=[
            pltpu.VMEM((LAYERS, 3, K, C), BF16),
            pltpu.VMEM((TH, TW, FR, C), BF16),
            pltpu.VMEM((FR * CELLS, C), F32),
            pltpu.VMEM((2, 2, TW, FR, C), BF16),
            pltpu.VMEM((2, 2, TH, FR, C), BF16),
            pltpu.VMEM((2, 4, 1, FR, C), BF16),
            pltpu.VMEM((2, 2, FR * TW, C), F32),
            pltpu.VMEM((2, 2, FR * (TH + 2) + 8, C), F32),
            pltpu.VMEM((inner, C), F32),
            pltpu.VMEM((inner, C), F32),
            pltpu.VMEM((inner, FR + 1, ROWS, C), F32),
            pltpu.VMEM((FR, ROWS, C), F32),
            pltpu.VMEM((FR + 2, 3, XROWS, C), F32),
            pltpu.VMEM((FR + 2, ROWS, K), BF16),
            pltpu.VMEM((2, 2, 56, C), F32),
            pltpu.VMEM((2, 2, 24, C), F32),
            pltpu.VMEM((4, 2, 16, C), F32),
            pltpu.VMEM((inner, 2, 2, 48, C), BF16),
            pltpu.VMEM((inner, 2, 2, 16, C), BF16),
            pltpu.VMEM((inner, 4, 2, FR, C), BF16),
            pltpu.VMEM((LAYERS, 2, ROWS, C), BF16),
            pltpu.VMEM((inner, 2, 2, 48, C), BF16),
            pltpu.VMEM((inner, 2, 2, 16, C), BF16),
            pltpu.VMEM((inner, 4, 2, FR, C), BF16),
            pltpu.VMEM((inner, 2, 48, C), BF16),
            pltpu.VMEM((inner, 2, 16, C), BF16),
            pltpu.VMEM((inner, 4, 2, FR, C), BF16),
            pltpu.VMEM((LAYERS, 2, ROWS, C), BF16),
            pltpu.VMEM((2, 2, 56, C), F32),
            pltpu.VMEM((2, 2, 24, C), F32),
            pltpu.VMEM((4, 2, 16, C), F32),
            pltpu.VMEM((inner, 2, C), F32),
            pltpu.VMEM((inner, n_space - 1, 2, C), F32),
            pltpu.VMEM((inner, n_space, 2, C), F32),
            pltpu.SemaphoreType.DMA((6,)),
            pltpu.SemaphoreType.DMA((LAYERS, 17)),
            pltpu.SemaphoreType.DMA((LAYERS, 17)),
            pltpu.SemaphoreType.DMA((inner, 2)),
            pltpu.SemaphoreType.DMA((inner, 2)),
            pltpu.SemaphoreType.REGULAR,
            pltpu.SemaphoreType.REGULAR,
        ],
        compiler_params=pltpu.CompilerParams(collective_id=0, has_side_effects=True, vmem_limit_bytes=48 << 20),
        cost_estimate=pl.CostEstimate(flops=1274019840, bytes_accessed=2900000, transcendentals=300000),
        name="conv_stack",
    )(*(pltpu.with_memory_space_constraint(value, pltpu.HBM) for value in arguments))
    return result[:, None]


def solution(mesh):
    placed = (P("tm", "space", None, None, None), P(), P(), P())
    return jax.shard_map(
        on_device,
        mesh=mesh,
        in_specs=placed,
        out_specs=P("tm", "space", None, None, None),
        check_vma=False,
    )
```

```python
import jax
import jax.numpy as jnp
from jax import lax
from jax.experimental import pallas as pl
from jax.experimental.pallas import tpu as pltpu
from jax.sharding import PartitionSpec as P

GROUPS = 32
TILE_COLS = 8
BANDS = 4
LAYERS = 3
EPS = 1e-05
F32 = jnp.float32
BF16 = jnp.bfloat16
MESH = pl.DeviceIdType.MESH

FR = 4
TH = 6
TW = 20
C = 128
CELLS = TH * TW
ROWS = 128
PAD = 8
XROWS = PAD + (TH + 2) * TW + 8
K = 9 * C
COUNT = BANDS * TH * TILE_COLS * TW * (C // GROUPS)


def dot(left, right):
    return jnp.dot(left, right, preferred_element_type=F32)


def roll(value, steps):
    return value if steps == 0 else pltpu.roll(value, steps % C, 1)


def pack_sums(total):
    lane = lax.broadcasted_iota(jnp.int32, (1, C), 1) % 4
    moved = {d: roll(total, d) for d in range(-3, 4)}
    first = jnp.zeros((1, C), F32)
    second = jnp.zeros((1, C), F32)
    for f in range(FR):
        group = (moved[f - 3] + moved[f - 2]) + (moved[f - 1] + moved[f])
        first = jnp.where(lane == f, group[f : f + 1], first)
        second = jnp.where(lane == f, group[4 + f : 5 + f], second)
    return jnp.concatenate([first, second], axis=0)


def unpack_sums(packed):
    lane = lax.broadcasted_iota(jnp.int32, (8, C), 1) % 4
    row = lax.broadcasted_iota(jnp.int32, (8, C), 0)
    spread = jnp.where(row < 4, packed[0:1], packed[1:2])
    gap = lane - row % 4
    result = spread
    for d in (-3, -2, -1, 1, 2, 3):
        result = jnp.where(gap == d, roll(spread, d), result)
    return result


def moments(packed, gain):
    sums = unpack_sums(packed) * (1.0 / COUNT)
    mean = sums[0:4]
    var = sums[4:8] - mean * mean
    return mean, lax.rsqrt(var + EPS) * gain


def side(column_part, top_corner, bottom_corner):
    row = lax.broadcasted_iota(jnp.int32, (8, C), 0)
    return jnp.where(row == 0, top_corner, jnp.where(row == TH + 1, bottom_corner, column_part))


FAR_FIRST = sorted(
    ((b, c) for b in range(-1, 3) for c in range(-3, 5) if (b, c) != (0, 0)), key=lambda o: (-abs(o[0]) - abs(o[1]), o)
)

STEPS = ((1, 0), (-1, 0), (0, 1), (0, -1), (-1, -1), (-1, 1), (1, -1), (1, 1))
CORNERS = ((0, 0), (0, TW - 1), (TH - 1, 0), (TH - 1, TW - 1))


def kernel(
    video,
    weights,
    gain_in,
    bias_in,
    out,
    w,
    vid,
    inter,
    first_row,
    first_col,
    first_corner,
    row_cells,
    col_cells,
    gains,
    biases,
    y,
    acc,
    xc,
    im,
    stage_row,
    stage_col,
    stage_corner,
    out_row,
    out_col,
    out_corner,
    out_halo,
    in_row,
    in_col,
    in_corner,
    next_row,
    next_col,
    next_corner,
    halo,
    rim_row,
    rim_col,
    rim_corner,
    packed,
    slots,
    prev_slots,
    load_sem,
    send_sem,
    recv_sem,
    stat_send,
    stat_recv,
    near_sem,
    ready_sem,
):
    tm = lax.axis_index("tm")
    space = lax.axis_index("space")
    n_tm = lax.axis_size("tm")
    n_space = lax.axis_size("space")
    band = space // TILE_COLS
    column = lax.rem(space, TILE_COLS)
    after = lax.rem(tm + 1, n_tm)
    before = lax.rem(tm + n_tm - 1, n_tm)

    bands = {b: lax.rem(band + b + BANDS, BANDS) * TILE_COLS for b in range(-1, 3)}
    columns = {c: lax.rem(column + c + TILE_COLS, TILE_COLS) for c in range(-3, 5)}
    tiles = {(b, c): bands[b] + columns[c] for b in bands for c in columns}

    def tile(b, c):
        return tiles[b, c]

    barrier = pltpu.get_barrier_semaphore()
    has_before = tm > 0
    has_after = tm < n_tm - 1

    @pl.when(has_before)
    def _():
        for step in STEPS[::-1] + ((0, 0),):
            pl.semaphore_signal(barrier, inc=1, device_id=(before, tile(*step)), device_id_type=MESH)

    for step in STEPS[::-1]:
        pl.semaphore_signal(barrier, inc=1, device_id=(tm, tile(*step)), device_id_type=MESH)

    loads = [pltpu.make_async_copy(video, vid, load_sem.at[0])]
    for layer in range(LAYERS):
        loads.append(pltpu.make_async_copy(weights.at[layer], w.at[layer], load_sem.at[1 + layer]))
    loads.append(pltpu.make_async_copy(gain_in, gains, load_sem.at[4]))
    loads.append(pltpu.make_async_copy(bias_in, biases, load_sem.at[5]))
    for copy in loads:
        copy.start()
    loads[0].wait()
    inter[...] = vid[...].astype(F32).reshape(FR * CELLS, C)
    for f in range(2):
        whole = jnp.concatenate([inter[pl.ds(2 + f, CELLS, stride=FR), :], jnp.zeros((ROWS - CELLS, C), F32)], axis=0)
        out_halo[0, f] = whole.astype(BF16)
    pl.semaphore_wait(barrier, len(STEPS) + jnp.where(has_after, len(STEPS) + 1, 0))

    def ends(t, k):
        if k == 8:
            return out_halo.at[t], halo.at[t]
        g, k = divmod(k, 9)
        s = t - 1
        if t == 0:
            if k < 2:
                return vid.at[(TH - 1, 0)[k]], first_row.at[g, k]
            if k < 4:
                return vid.at[:, (TW - 1, 0)[k - 2]], first_col.at[g, k - 2]
            h, c = CORNERS[k - 4]
            return vid.at[h, pl.ds(c, 1)], first_corner.at[g, 7 - k]
        if k < 2:
            return (out_row.at[s, k, 1], next_row.at[s, k]) if g else (out_row.at[s, k], in_row.at[s, k])
        if k < 4:
            k = k - 2
            return (out_col.at[s, k, 1], next_col.at[s, k]) if g else (out_col.at[s, k], in_col.at[s, k])
        return out_corner.at[s, k - 4], (next_corner if g else in_corner).at[s, 7 - k]

    def message(t, k):
        source, land = ends(t, k)
        step = (0, 0) if k == 8 else STEPS[k % 9]
        return pltpu.make_async_remote_copy(
            src_ref=source,
            dst_ref=land,
            send_sem=send_sem.at[t, k],
            recv_sem=recv_sem.at[t, k],
            device_id=(tm if k < 8 else after, tile(*step)),
            device_id_type=MESH,
        )

    def send_all(t):
        for k in range(7, -1, -1):
            message(t, k).start()

        @pl.when(has_after)
        def _():
            for k in (16, 15, 14, 13, 12, 11, 10, 9, 8):
                message(t, k).start()

    def fill(slot, own, top, bottom, left_side, right_side):
        for c in range(3):
            off = PAD + 1 - c
            xc[slot, c, off : off + TW, :] = top
            xc[slot, c, off + TW : off + TW + CELLS, :] = own
            xc[slot, c, off + TW + CELLS : off + 2 * TW + CELLS, :] = bottom
        xc[slot, 0, pl.ds(PAD, TH + 2, stride=TW), :] = left_side
        xc[slot, 2, pl.ds(PAD + TW - 1, TH + 2, stride=TW), :] = right_side
        zeros = jnp.zeros((ROWS - CELLS, C), F32)
        for b in range(3):
            for c in range(3):
                start = PAD + b * TW
                part = jnp.concatenate([xc[slot, c, start : start + CELLS, :], zeros], axis=0)
                tap = b * 3 + c
                im[slot, :, tap * C : (tap + 1) * C] = part.astype(BF16)

    row8 = lax.broadcasted_iota(jnp.int32, (8, C), 0)
    keep_rows = ((row8 > 0) | (band > 0)) & ((row8 < TH + 1) | (band < BANDS - 1))
    keep_left = keep_rows & (column > 0)
    keep_right = keep_rows & (column < TILE_COLS - 1)

    def frame(slot, parts, act, keep):
        own, top, bottom, left_side, right_side = (act(*part) for part in parts)
        fill(
            slot,
            keep(own),
            keep(jnp.where(band > 0, top, 0.0)),
            keep(jnp.where(band < BANDS - 1, bottom, 0.0)),
            keep(jnp.where(keep_left, left_side, 0.0)),
            keep(jnp.where(keep_right, right_side, 0.0)),
        )

    def same(value, shift=None):
        return value

    def later(value):
        return jnp.where(tm > 0, value, 0.0)

    def split(g, f):
        return (
            (row_cells[g, 0, pl.ds(f, TW, stride=FR), :], None),
            (row_cells[g, 1, pl.ds(f, TW, stride=FR), :], None),
            (col_cells[g, 0, pl.ds(f, TH + 2, stride=FR), :], None),
            (col_cells[g, 1, pl.ds(f, TH + 2, stride=FR), :], None),
        )

    def unpack_rims(g):
        for i in range(2):
            row_cells[g, i] = first_row[g, i].astype(F32).reshape(FR * TW, C)
            col_cells[g, i, FR : FR * (TH + 1), :] = first_col[g, i].astype(F32).reshape(FR * TH, C)
            col_cells[g, i, 0:FR, :] = first_corner[g, i].astype(F32).reshape(FR, C)
            col_cells[g, i, FR * (TH + 1) : FR * (TH + 2), :] = first_corner[g, 2 + i].astype(F32).reshape(FR, C)

    def rims_of(p, f):
        lo = f * TW
        own = 2 * p + f
        rims = [(rim_row[i, p, lo : lo + TW, :], rim_row[i, p, 2 * TW + f : 2 * TW + f + 1, :]) for i in range(2)]
        for i in range(2):
            part = rim_col[i, p, 8 * f : 8 * f + 8, :]
            upper, lower = ((rim_corner[k, 0, own : own + 1, :], rim_corner[k, 1, own : own + 1, :]) for k in (i, 2 + i))
            rims.append((side(part, upper[0], lower[0]), side(part[0:1], upper[1], lower[1])))
        return rims

    for t in range(LAYERS):
        s = t - 1
        if t == 0:
            send_all(0)
        else:
            value = y[s, 0:FR]
            sums = [jnp.sum(value[f], axis=0, keepdims=True) for f in range(FR)]
            squares = [jnp.sum(value[f] * value[f], axis=0, keepdims=True) for f in range(FR)]
            packed[s] = pack_sums(jnp.concatenate(sums + squares, axis=0))

            def tell(k, offset, device, buffer, mine, s=s):
                pltpu.make_async_remote_copy(
                    src_ref=packed.at[s],
                    dst_ref=buffer.at[s, k],
                    send_sem=stat_send.at[s, mine],
                    recv_sem=stat_recv.at[s, mine],
                    device_id=(device, tile(*offset)),
                    device_id_type=MESH,
                ).start()

            for k, offset in enumerate(FAR_FIRST):
                tell(k, offset, tm, slots, 0)

            @pl.when(has_after)
            def _(tell=tell, t=t):
                if t == 1:
                    pl.semaphore_wait(ready_sem, 1)
                for k, offset in enumerate(FAR_FIRST + [(0, 0)]):
                    tell(k, offset, after, prev_slots, 1)

            for f in range(FR):
                off = (sums[f] * (1.0 / CELLS)).astype(BF16).astype(F32)
                p, lo = f // 2, f % 2
                for i, first in enumerate((CELLS - TW, 0)):
                    stage_row[i, p, lo * TW : (lo + 1) * TW, :] = y[s, f, first : first + TW, :] - off
                    stage_row[i, p, 2 * TW + lo : 2 * TW + lo + 1, :] = off
                for i, first in enumerate((TW - 1, 0)):
                    stage_col[i, p, 8 * lo : 8 * lo + 8, :] = jnp.broadcast_to(off, (8, C))
                    stage_col[i, p, 8 * lo + 1 : 8 * lo + 1 + TH, :] = y[s, f, pl.ds(first, TH, stride=TW), :] - off
                for k, (h, c) in enumerate(CORNERS):
                    cell = h * TW + c
                    stage_corner[k, 0, f : f + 1, :] = y[s, f, cell : cell + 1, :] - off
                    stage_corner[k, 1, f : f + 1, :] = off
                if p == 1:
                    whole = jnp.concatenate([y[s, f, 0:CELLS, :] - off, jnp.broadcast_to(off, (ROWS - CELLS, C))], axis=0)
                    out_halo[t, lo] = whole.astype(BF16)
            out_row[s] = stage_row[:, :, 0:48, :].astype(BF16)
            out_col[s] = stage_col[:, :, 0:16, :].astype(BF16)
            out_corner[s] = stage_corner[:, :, 0:FR, :].astype(BF16)
            send_all(t)

        for k in range(8):
            message(t, k).wait_recv()
        loads[1 + t].wait()

        if t == 0:
            for step in ((0, 2), (0, -2)):
                pl.semaphore_signal(near_sem, inc=1, device_id=(tm, tile(*step)), device_id_type=MESH)
            unpack_rims(0)
            for f in range(FR):
                frame(2 + f, [(inter[pl.ds(f, CELLS, stride=FR), :], None), *split(0, f)], same, same)
        else:
            if t == 1:
                loads[4].wait()
                loads[5].wait()
            gain = gains[s : s + 1, :]
            bias = biases[s : s + 1, :]

            def act_of(f, stats, bias=bias):
                mean, scale = stats

                def act(value, off=0.0):
                    v = (value + (off - mean[f : f + 1])) * scale[f : f + 1] + bias
                    return v / (1.0 + jnp.exp(-v))

                return act

            rim_row[:, :, 0:48, :] = in_row[s].astype(F32)
            rim_col[:, :, 0:16, :] = in_col[s].astype(F32)
            rim_corner[:, :, 0:FR, :] = in_corner[s].astype(F32)
            pltpu.make_async_copy(slots.at[s], slots.at[s], stat_recv.at[s, 0]).wait()
            stats = moments(packed[s] + jnp.sum(slots[s], axis=0), gain)
            for f in range(FR):
                frame(2 + f, [(y[s, f, 0:CELLS, :],), *rims_of(f // 2, f % 2)], act_of(f, stats), same)

        w21 = jnp.concatenate([w[t, 2], w[t, 1]], axis=1)
        two = dot(im[2:5].reshape(3 * ROWS, K), w21).reshape(3, ROWS, 2 * C)
        one = dot(im[5], w[t, 2])
        old = dot(im[2:4].reshape(2 * ROWS, K), w[t, 0]).reshape(2, ROWS, C)
        acc[0] = two[0, :, :C]
        acc[1] = two[0, :, C:] + two[1, :, :C]
        acc[2] = two[1, :, C:] + two[2, :, :C] + old[0]
        acc[3] = two[2, :, C:] + one + old[1]

        if t == 0:
            pl.semaphore_wait(near_sem, 2)

        @pl.when(has_before)
        def _(s=s, t=t):
            for k in range(8, 17):
                message(t, k).wait_recv()
            if t == 0:
                pl.semaphore_signal(ready_sem, inc=1, device_id=(before, space), device_id_type=MESH)
            else:
                pltpu.make_async_copy(prev_slots.at[s], prev_slots.at[s], stat_recv.at[s, 1]).wait()

        if t == 0:
            unpack_rims(1)
            for f in range(2):
                frame(f, [(halo[0, f].astype(F32)[0:CELLS],), *split(1, 2 + f)], same, later)
        else:
            for i in range(2):
                rim_row[i, 1, 0:48, :] = next_row[s, i].astype(F32)
                rim_col[i, 1, 0:16, :] = next_col[s, i].astype(F32)
            rim_corner[:, :, 0:FR, :] = next_corner[s].astype(F32)
            stats = moments(jnp.sum(prev_slots[s], axis=0), gain)
            for f in range(2):
                whole = halo[t, f].astype(F32)
                frame(f, [(whole[0:CELLS], whole[CELLS : CELLS + 1]), *rims_of(1, f)], act_of(2 + f, stats), later)
        w10 = jnp.concatenate([w[t, 1], w[t, 0]], axis=1)
        near = dot(im[1], w10)
        far = dot(im[0], w[t, 0])
        result = [acc[0] + near[:, :C] + far, acc[1] + near[:, C:], acc[2], acc[3]]
        for f in range(FR):
            if t < LAYERS - 1:
                y[t, f] = result[f]
            else:
                for h in range(TH):
                    out[f, h] = result[f][h * TW : (h + 1) * TW].astype(BF16)

    for t in range(LAYERS):
        for k in range(8):
            message(t, k).wait_send()
    for s in range(LAYERS - 1):
        pltpu.make_async_copy(slots.at[s], slots.at[s], stat_send.at[s, 0]).wait()

    @pl.when(has_after)
    def _():
        for t in range(LAYERS):
            for k in range(8, 17):
                message(t, k).wait_send()
        for s in range(LAYERS - 1):
            pltpu.make_async_copy(prev_slots.at[s], prev_slots.at[s], stat_send.at[s, 1]).wait()


def on_device(video, conv_weight, norm_gain, norm_bias):
    n_space = lax.axis_size("space")
    inner = LAYERS - 1
    arguments = (
        video.reshape(FR, TH, TW, C).transpose(1, 2, 0, 3),
        conv_weight.reshape(LAYERS, 3, K, C),
        norm_gain,
        norm_bias,
    )
    result = pl.pallas_call(
        kernel,
        out_shape=jax.ShapeDtypeStruct((FR, TH, TW, C), BF16),
        in_specs=[pl.BlockSpec(memory_space=pltpu.HBM)] * 4,
        out_specs=pl.BlockSpec(memory_space=pltpu.VMEM),
        scratch_shapes=[
            pltpu.VMEM((LAYERS, 3, K, C), BF16),
            pltpu.VMEM((TH, TW, FR, C), BF16),
            pltpu.VMEM((FR * CELLS, C), F32),
            pltpu.VMEM((2, 2, TW, FR, C), BF16),
            pltpu.VMEM((2, 2, TH, FR, C), BF16),
            pltpu.VMEM((2, 4, 1, FR, C), BF16),
            pltpu.VMEM((2, 2, FR * TW, C), F32),
            pltpu.VMEM((2, 2, FR * (TH + 2) + 8, C), F32),
            pltpu.VMEM((inner, C), F32),
            pltpu.VMEM((inner, C), F32),
            pltpu.VMEM((inner, FR + 1, ROWS, C), F32),
            pltpu.VMEM((FR, ROWS, C), F32),
            pltpu.VMEM((FR + 2, 3, XROWS, C), F32),
            pltpu.VMEM((FR + 2, ROWS, K), BF16),
            pltpu.VMEM((2, 2, 56, C), F32),
            pltpu.VMEM((2, 2, 24, C), F32),
            pltpu.VMEM((4, 2, 16, C), F32),
            pltpu.VMEM((inner, 2, 2, 48, C), BF16),
            pltpu.VMEM((inner, 2, 2, 16, C), BF16),
            pltpu.VMEM((inner, 4, 2, FR, C), BF16),
            pltpu.VMEM((LAYERS, 2, ROWS, C), BF16),
            pltpu.VMEM((inner, 2, 2, 48, C), BF16),
            pltpu.VMEM((inner, 2, 2, 16, C), BF16),
            pltpu.VMEM((inner, 4, 2, FR, C), BF16),
            pltpu.VMEM((inner, 2, 48, C), BF16),
            pltpu.VMEM((inner, 2, 16, C), BF16),
            pltpu.VMEM((inner, 4, 2, FR, C), BF16),
            pltpu.VMEM((LAYERS, 2, ROWS, C), BF16),
            pltpu.VMEM((2, 2, 56, C), F32),
            pltpu.VMEM((2, 2, 24, C), F32),
            pltpu.VMEM((4, 2, 16, C), F32),
            pltpu.VMEM((inner, 2, C), F32),
            pltpu.VMEM((inner, n_space - 1, 2, C), F32),
            pltpu.VMEM((inner, n_space, 2, C), F32),
            pltpu.SemaphoreType.DMA((6,)),
            pltpu.SemaphoreType.DMA((LAYERS, 17)),
            pltpu.SemaphoreType.DMA((LAYERS, 17)),
            pltpu.SemaphoreType.DMA((inner, 2)),
            pltpu.SemaphoreType.DMA((inner, 2)),
            pltpu.SemaphoreType.REGULAR,
            pltpu.SemaphoreType.REGULAR,
        ],
        compiler_params=pltpu.CompilerParams(collective_id=0, has_side_effects=True, vmem_limit_bytes=48 << 20),
        cost_estimate=pl.CostEstimate(flops=1274019840, bytes_accessed=2900000, transcendentals=300000),
        name="conv_stack",
    )(*(pltpu.with_memory_space_constraint(value, pltpu.HBM) for value in arguments))
    return result[:, None]


def solution(mesh):
    placed = (P("tm", "space", None, None, None), P(), P(), P())
    return jax.shard_map(
        on_device,
        mesh=mesh,
        in_specs=placed,
        out_specs=P("tm", "space", None, None, None),
        check_vma=False,
    )
```
